128 devices in a mesh: ctx: 64 (over z, x, y), kvh: 2 (over core).
Axes of the slice: x: 4, y: 4, z: 4, core: 2. Of those that a mesh axis runs over, the one named last changes fastest.
Arguments:
- hidden_in: bfloat16 [4, 2, 8192], replicated, may hold values from -0.0625 to 0.0625
- attn_gain: bfloat16 [8192], replicated, may hold values from 0.099609375 to 1.8984375
- q_weight: bfloat16 [8192, 8192], P('ctx', 'kvh'), may hold values from -1 to 1
- k_weight: bfloat16 [8192, 1024], P('ctx', 'kvh'), may hold values from -1 to 1
- v_weight: bfloat16 [8192, 1024], P('ctx', 'kvh'), may hold values from -0.00390625 to 0.00390625
- key_cache: bfloat16 [4, 65536, 8, 128], P(None, 'ctx', 'kvh'), may hold values from -82 to 82, as said below
- value_cache: bfloat16 [4, 65536, 8, 128], P(None, 'ctx', 'kvh'), may hold values from -6 to 6
- lengths: int32 [4], replicated, may hold values from 16384 to 65534, as said below
- positions: int32 [4], replicated, may hold values from 16384 to 131070, as said below
- o_weight: bfloat16 [8192, 8192], P('kvh', 'ctx'), may hold values from -0.0625 to 0.0625
- ffn_gain: bfloat16 [8192], replicated, may hold values from 0.099609375 to 1.8984375
- gate_weight: bfloat16 [8192, 28672], P(None, ('ctx', 'kvh')), may hold values from -0.0625 to 0.0625
- up_weight: bfloat16 [8192, 28672], P(None, ('ctx', 'kvh')), may hold values from -0.0625 to 0.0625
- down_weight: bfloat16 [28672, 8192], P(('ctx', 'kvh')), may hold values from -0.125 to 0.125
Outputs:
- output: bfloat16 [4, 2, 8192], P(None, None, ('ctx', 'kvh'))
The draws below stay inside these ranges and needn't reach their ends.
Inputs may be any that keep to these rules, and one draw needn't show every extreme that they name: Slots below lengths[b] hold row b's cached keys and values; its new tokens go to slots lengths[b] and lengths[b] + 1. positions[b] >= lengths[b]. `key_cache`: cached keys are already rotated for their positions.
All inputs are finite; a program needn't handle non-finite values.
Results may differ from the reference program's by a relative error of at most 0.035.
Values may be sent and summed in bfloat16 or wider, within the bound.
No kernel may reach another device: no remote copies, remote signals or barrier semaphores. Data moves between devices by JAX's collectives and lax.ppermute only.
A program may use at most 128 MiB of HBM per device.

```python
import jax
import jax.numpy as jnp
from jax import lax

D = 8192
FF = 28672
QH = 64
KVH = 8
HD = 128
ROWS = 4
STEPS = 2
CTX_DEV = 1024
CTX = 65536


def length_draw(key):
    order_key, length_key, evict_key = jax.random.split(key, 3)
    row_order = jax.random.permutation(order_key, ROWS)
    row_ids = jnp.arange(ROWS, dtype=jnp.int32)
    longest = row_ids == row_order[0]
    shortest = row_ids == row_order[1]
    lengths = jax.random.randint(length_key, (ROWS,), CTX // 4, CTX - 1, dtype=jnp.int32)
    lengths = jnp.where(longest, CTX - 2, jnp.where(shortest, CTX // 4, lengths))
    evicted = jax.random.randint(evict_key, (ROWS,), 0, CTX + 1, dtype=jnp.int32)
    evicted = jnp.where(longest, CTX, jnp.where(shortest, 0, evicted))
    return (lengths, lengths + evicted)


def projection_draw(key):
    normal_key = jax.random.fold_in(key, 0)
    normal_part = jax.random.truncated_normal(normal_key, -4.0, 4.0, (D, QH * HD), jnp.float32)
    return normal_part


def draw_lengths(key, part):
    shared = length_draw(key)
    return shared[0]


def draw_positions(key, part):
    shared = length_draw(key)
    return shared[1]


def draw_q_weight(key, part):
    normal_part = projection_draw(key)
    entries = normal_part
    return (entries * (1.5 * D ** (-0.5))).astype(jnp.bfloat16)


def draw_k_weight(key, part):
    normal_part = projection_draw(key)
    entries = normal_part
    entries = entries.reshape(D, KVH, QH // KVH, HD)[:, :, 0, :].reshape(D, KVH * HD)
    return (entries * (1.5 * D ** (-0.5))).astype(jnp.bfloat16)


def draw_key_cache(key, part):
    key = jax.random.fold_in(key, 7)
    entry_key = jax.random.fold_in(key, 1)
    entries = jax.random.truncated_normal(entry_key, -6.0, 6.0, (ROWS, CTX, KVH, HD), jnp.float32)
    return entries.astype(jnp.bfloat16)


def with_spikes(drawn, own_key, source, target, blocks, factor):
    owner, partner = [(jnp.arange(drawn.shape[dim]) // (drawn.shape[dim] // blocks)).reshape([-1 if axis == dim else 1 for axis in range(drawn.ndim)]) for dim in (source, target)]
    chosen = jax.random.permutation(own_key, blocks)[partner]
    strong = (owner == chosen) | (owner == (partner + blocks // 2) % blocks)
    return jnp.where(strong, factor * drawn, drawn)


def block_scale(rng, shape, pieces, smallest, high):
    factor_of, own = 1.0, jax.random.fold_in(rng, 6)
    for dim, blocks in pieces:
        heights = jnp.exp(jax.random.uniform(jax.random.fold_in(own, dim), (blocks,), jnp.float32, smallest / len(pieces), high / len(pieces)))
        factor_of = factor_of * jnp.repeat(heights, shape[dim] // blocks).reshape([-1 if axis == dim else 1 for axis in range(len(shape))])
    return factor_of


def scatter_about(own_key, dims, width, reach, cuts=(), kind=jnp.bfloat16):
    gain = block_scale(own_key, dims, cuts, -0.22, 0.18) if cuts else 1.0
    values = jax.random.normal(own_key, dims, jnp.float32) * width * gain
    return jnp.minimum(jnp.maximum(values, -reach), reach).astype(kind)


def noise_with(rng, dims, width, bound, cuts, heavy, kind=jnp.bfloat16):
    result = width * jax.random.normal(rng, dims, jnp.float32)
    if cuts:
        result = result * block_scale(rng, dims, cuts, -0.22, 0.18)
    return jnp.clip(with_spikes(result, jax.random.fold_in(rng, 3), *heavy), -bound, bound).astype(kind)


def setup_inputs(seed: int = 0) -> dict:
    key_list = jax.random.split(jax.random.key(seed), 15)
    return {
        "hidden_in": scatter_about(key_list[0], (ROWS, STEPS, D), 0.01, 0.0625),
        "attn_gain": jnp.clip(1.0 + 0.18 * jax.random.normal(key_list[1], (D,), jnp.float32), 0.099609375, 1.8984375).astype(jnp.bfloat16),
        "q_weight": draw_q_weight(jax.random.fold_in(key_list[14], 71), 0),
        "k_weight": draw_k_weight(jax.random.fold_in(key_list[14], 71), 0),
        "v_weight": scatter_about(key_list[4], (D, KVH * HD), (256 * D) ** -0.5, 0.00390625, ((0, 64), (1, 2))),
        "key_cache": draw_key_cache(jax.random.fold_in(key_list[14], 71), 0),
        "value_cache": scatter_about(key_list[6], (ROWS, CTX, KVH, HD), 1.0, 6.0, ((1, 64), (2, 2))),
        "lengths": draw_lengths(jax.random.fold_in(key_list[14], 71), 0),
        "positions": draw_positions(jax.random.fold_in(key_list[14], 71), 0),
        "o_weight": scatter_about(key_list[9], (QH * HD, D), (QH * HD) ** -0.5, 0.0625, ((0, 2), (1, 64))),
        "ffn_gain": jnp.clip(1.0 + 0.18 * jax.random.normal(key_list[10], (D,), jnp.float32), 0.099609375, 1.8984375).astype(jnp.bfloat16),
        "gate_weight": scatter_about(key_list[11], (D, FF), D ** -0.5, 0.0625, ((1, 128),)),
        "up_weight": scatter_about(key_list[12], (D, FF), D ** -0.5, 0.0625, ((1, 128),)),
        "down_weight": noise_with(key_list[13], (FF, D), FF ** -0.5, 0.125, ((0, 128),), (0, 1, 128, 5.5)),
    }


def rms_scale(values, gain_row):
    values = values.astype(jnp.float32)
    spread = lax.optimization_barrier(jnp.mean(values * values, axis=-1, keepdims=True))
    return values * lax.rsqrt(spread + 1e-05) * gain_row.astype(jnp.float32)

def rotary_tables(places, head_dim):
    half_dim = head_dim // 2
    ladder = jnp.arange(half_dim, dtype=jnp.float32) * (2.0 / head_dim)
    frequency = jnp.exp(-ladder * jnp.log(500000.0))
    angles = places[:, None] * frequency[None, :]
    return (jnp.cos(angles), jnp.sin(angles))

def rotate_pair(values, cosine, sine_part):
    half_dim = values.shape[-1] // 2
    first_half = values[..., :half_dim]
    second_half = values[..., half_dim:]
    cosine = cosine[:, None, :]
    sine_part = sine_part[:, None, :]
    return jnp.concatenate([first_half * cosine - second_half * sine_part, second_half * cosine + first_half * sine_part], axis=-1)

def attend_row(row_items):
    queries, new_keys, new_values, keys_row, values_row, length = row_items
    group_size = QH // KVH
    zero_index = jnp.zeros((), jnp.int32)
    start_slot = length.astype(jnp.int32)
    keys_row = lax.dynamic_update_slice(keys_row, new_keys, (start_slot, zero_index, zero_index))
    values_row = lax.dynamic_update_slice(values_row, new_values, (start_slot, zero_index, zero_index))
    blocks = CTX // CTX_DEV
    key_blocks = keys_row.reshape(blocks, CTX_DEV, KVH, HD).astype(jnp.float32)
    value_blocks = values_row.reshape(blocks, CTX_DEV, KVH, HD).astype(jnp.float32)
    scores = jnp.einsum('kmd,nckd->nkmc', queries.astype(jnp.float32), key_blocks) * HD ** (-0.5)
    slot_ids = jnp.arange(CTX, dtype=jnp.int32).reshape(blocks, 1, 1, CTX_DEV)
    step_of = (jnp.arange(STEPS * group_size, dtype=jnp.int32) // group_size).reshape(1, 1, STEPS * group_size, 1)
    visible = slot_ids < start_slot + step_of + 1
    masked = jnp.where(visible, scores, -1e+30)
    block_max = lax.optimization_barrier(jnp.max(masked, axis=-1))
    weights = jnp.where(visible, jnp.exp(masked - block_max[..., None]), 0.0)
    block_total = lax.optimization_barrier(jnp.sum(weights, axis=-1))
    rounded = lax.optimization_barrier(weights.astype(jnp.bfloat16)).astype(jnp.float32)
    block_out = jnp.einsum('nkmc,nckd->nkmd', rounded, value_blocks)
    overall = lax.optimization_barrier(jnp.max(block_max, axis=0))
    factor = jnp.exp(block_max - overall[None])
    total_sum = lax.optimization_barrier(jnp.sum(block_total * factor, axis=0))
    merged = lax.optimization_barrier(jnp.sum(block_out * factor[..., None], axis=0))
    return (merged / total_sum[..., None]).astype(jnp.bfloat16)

def reference(hidden_in, attn_gain, q_weight, k_weight, v_weight, key_cache, value_cache, lengths, positions, o_weight, ffn_gain, gate_weight, up_weight, down_weight):
    tokens = ROWS * STEPS
    group_size = QH // KVH
    flat_in = hidden_in.reshape(tokens, D)
    normed = rms_scale(flat_in, attn_gain).astype(jnp.bfloat16)
    query_sum = jnp.dot(normed, q_weight, preferred_element_type=jnp.float32)
    key_sum = jnp.dot(normed, k_weight, preferred_element_type=jnp.float32)
    value_sum = jnp.dot(normed, v_weight, preferred_element_type=jnp.float32)
    places = (positions[:, None] + jnp.arange(STEPS, dtype=jnp.int32)[None, :]).reshape(tokens).astype(jnp.float32)
    cosine, sine_part = rotary_tables(places, HD)
    queries = rotate_pair(query_sum.reshape(tokens, QH, HD), cosine, sine_part).astype(jnp.bfloat16)
    queries = queries.reshape(ROWS, STEPS, KVH, group_size, HD).transpose(0, 2, 1, 3, 4).reshape(ROWS, KVH, STEPS * group_size, HD)
    new_keys = rotate_pair(key_sum.reshape(tokens, KVH, HD), cosine, sine_part).astype(jnp.bfloat16).reshape(ROWS, STEPS, KVH, HD)
    new_values = value_sum.astype(jnp.bfloat16).reshape(ROWS, STEPS, KVH, HD)
    attended = lax.map(attend_row, (queries, new_keys, new_values, key_cache, value_cache, lengths))
    attended = attended.reshape(ROWS, KVH, STEPS, group_size, HD).transpose(0, 2, 1, 3, 4).reshape(tokens, QH * HD)
    attn_out = jnp.dot(attended, o_weight, preferred_element_type=jnp.float32)
    residual = (flat_in.astype(jnp.float32) + attn_out).astype(jnp.bfloat16)
    ffn_input = rms_scale(residual, ffn_gain).astype(jnp.bfloat16)
    gate_val = jnp.dot(ffn_input, gate_weight, preferred_element_type=jnp.float32)
    up_val = jnp.dot(ffn_input, up_weight, preferred_element_type=jnp.float32)
    inner_act = (jax.nn.silu(gate_val) * up_val).astype(jnp.bfloat16)
    output = residual.astype(jnp.float32) + jnp.dot(inner_act, down_weight, preferred_element_type=jnp.float32)
    return output.astype(jnp.bfloat16).reshape(ROWS, STEPS, D)
```

```python
import jax
import jax.numpy as jnp
from jax import lax
from jax.sharding import PartitionSpec as P


def rms_scale(values, gain_row):
    values = values.astype(jnp.float32)
    spread = jnp.mean(values * values, axis=-1, keepdims=True)
    return values * lax.rsqrt(spread + 1e-05) * gain_row.astype(jnp.float32)


def rotary_tables(places, head_dim):
    half_dim = head_dim // 2
    ladder = jnp.arange(half_dim, dtype=jnp.float32) * (2.0 / head_dim)
    frequency = jnp.exp(-ladder * jnp.log(500000.0))
    angles = places[:, None] * frequency[None, :]
    return (jnp.cos(angles), jnp.sin(angles))


def exchange(blocks):
    return lax.all_to_all(blocks, "ctx", 0, 0, tiled=True)


def spread_block(block):
    ctx_count = lax.axis_size("ctx")
    return exchange(jnp.broadcast_to(block[None], (ctx_count,) + block.shape))


def core_sum(values):
    return values + lax.ppermute(values, "kvh", [(0, 1), (1, 0)])


def shards(
    hidden_in,
    attn_gain,
    q_weight,
    k_weight,
    v_weight,
    key_cache,
    value_cache,
    lengths,
    positions,
    o_weight,
    ffn_gain,
    gate_weight,
    up_weight,
    down_weight,
):
    row_count, step_count, model_width = hidden_in.shape
    tokens = row_count * step_count
    head_dim = key_cache.shape[3]
    local_kv = key_cache.shape[2]
    span_len = key_cache.shape[1]
    local_heads = q_weight.shape[1] // head_dim
    group_size = local_heads // local_kv
    slice_width = q_weight.shape[0]
    shard_index = lax.axis_index("ctx")
    kvh_index = lax.axis_index("kvh")
    ctx_count = lax.axis_size("ctx")
    half_dim = head_dim // 2

    flat_in = hidden_in.reshape(tokens, model_width)
    normed = rms_scale(flat_in, attn_gain).astype(jnp.bfloat16)
    own_cols = lax.dynamic_slice_in_dim(normed, shard_index * slice_width, slice_width, 1)
    query_part = jnp.dot(own_cols, q_weight, preferred_element_type=jnp.float32)
    key_part = jnp.dot(own_cols, k_weight, preferred_element_type=jnp.float32)
    value_part = jnp.dot(own_cols, v_weight, preferred_element_type=jnp.float32)
    head_blocks = jnp.concatenate(
        [
            part.reshape(tokens, -1, head_dim).transpose(1, 0, 2)
            for part in (query_part, key_part, value_part)
        ],
        axis=0,
    )
    qk_heads = local_heads + local_kv
    all_heads = qk_heads + local_kv
    head_blocks = jnp.pad(head_blocks, ((0, ctx_count - all_heads), (0, 0), (0, 0)))
    head_sum = jnp.sum(exchange(head_blocks), axis=0)

    places = (
        (positions[:, None] + jnp.arange(step_count, dtype=jnp.int32)[None, :])
        .reshape(tokens)
        .astype(jnp.float32)
    )
    cosine, sine_part = rotary_tables(places, head_dim)
    turned = shard_index < qk_heads
    cosine = jnp.where(turned, cosine, 1.0)
    sine_part = jnp.where(turned, sine_part, 0.0)
    first_half = head_sum[:, :half_dim]
    second_half = head_sum[:, half_dim:]
    head_done = jnp.concatenate(
        [
            first_half * cosine - second_half * sine_part,
            second_half * cosine + first_half * sine_part,
        ],
        axis=-1,
    ).astype(jnp.bfloat16)
    heads = spread_block(head_done)

    queries = (
        heads[:local_heads]
        .reshape(local_kv, group_size, row_count, step_count, head_dim)
        .transpose(2, 0, 1, 3, 4)
        .reshape(row_count, local_kv, group_size * step_count, head_dim)
    )
    new_keys = (
        heads[local_heads:qk_heads]
        .reshape(local_kv, row_count, step_count, head_dim)
        .transpose(1, 2, 0, 3)
    )
    new_values = (
        heads[qk_heads:all_heads]
        .reshape(local_kv, row_count, step_count, head_dim)
        .transpose(1, 2, 0, 3)
    )

    scale_val = head_dim ** (-0.5)
    cached_scores = (
        jnp.einsum("bkmd,bckd->bkmc", queries, key_cache, preferred_element_type=jnp.float32)
        * scale_val
    )
    fresh_scores = (
        jnp.einsum("bkmd,bskd->bkms", queries, new_keys, preferred_element_type=jnp.float32)
        * scale_val
    )
    slot_ids = shard_index * span_len + jnp.arange(span_len, dtype=jnp.int32)
    cached_ok = (slot_ids[None, :] < lengths[:, None])[:, None, None, :]
    step_ids = jnp.arange(step_count, dtype=jnp.int32)
    step_of = jnp.arange(step_count * group_size, dtype=jnp.int32) % step_count
    owned_new = (lengths[:, None] + step_ids[None, :]) // span_len == shard_index
    fresh_ok = owned_new[:, None, None, :] & (
        step_ids[None, None, None, :] <= step_of[None, None, :, None]
    )
    cached_masked = jnp.where(cached_ok, cached_scores, -1e30)
    fresh_masked = jnp.where(fresh_ok, fresh_scores, -1e30)
    local_max = jnp.maximum(jnp.max(cached_masked, axis=-1), jnp.max(fresh_masked, axis=-1))
    cached_weights = jnp.where(cached_ok, jnp.exp(cached_masked - local_max[..., None]), 0.0)
    fresh_weights = jnp.where(fresh_ok, jnp.exp(fresh_masked - local_max[..., None]), 0.0)
    local_total = jnp.sum(cached_weights, axis=-1) + jnp.sum(fresh_weights, axis=-1)
    local_out = jnp.einsum(
        "bkmc,bckd->bkmd",
        cached_weights.astype(jnp.bfloat16),
        value_cache,
        preferred_element_type=jnp.float32,
    )
    local_out = local_out + jnp.einsum(
        "bkms,bskd->bkmd",
        fresh_weights.astype(jnp.bfloat16),
        new_values,
        preferred_element_type=jnp.float32,
    )

    share = local_heads * tokens // ctx_count

    def by_head(values):
        width = values.shape[-1]
        return (
            values.reshape(row_count, local_kv, group_size, step_count, width)
            .transpose(1, 2, 0, 3, 4)
            .reshape(ctx_count, share, width)
        )

    stats = jnp.concatenate(
        [
            jnp.broadcast_to(local_max[..., None], local_max.shape + (half_dim,)),
            jnp.broadcast_to(local_total[..., None], local_total.shape + (half_dim,)),
        ],
        axis=-1,
    )
    partials = exchange(jnp.concatenate([by_head(local_out), by_head(stats)], axis=1))
    out_parts = partials[:, :share]
    max_parts = partials[:, share:, :1]
    total_parts = partials[:, share:, half_dim : half_dim + 1]
    factor = jnp.exp(max_parts - jnp.max(max_parts, axis=0, keepdims=True))
    total_sum = jnp.sum(total_parts * factor, axis=0)
    out_sum = jnp.sum(out_parts * factor, axis=0)
    attended = spread_block((out_sum / total_sum).astype(jnp.bfloat16))
    attended = (
        attended.reshape(local_heads, tokens, head_dim)
        .transpose(1, 0, 2)
        .reshape(tokens, local_heads * head_dim)
    )

    attn_cols = core_sum(jnp.dot(attended, o_weight, preferred_element_type=jnp.float32))
    own_input = lax.dynamic_slice_in_dim(flat_in, shard_index * slice_width, slice_width, 1)
    residual_cols = (own_input.astype(jnp.float32) + attn_cols).astype(jnp.bfloat16)
    residual = spread_block(residual_cols).transpose(1, 0, 2).reshape(tokens, model_width)

    ffn_input = rms_scale(residual, ffn_gain).astype(jnp.bfloat16)
    gate_val = jnp.dot(ffn_input, gate_weight, preferred_element_type=jnp.float32)
    up_val = jnp.dot(ffn_input, up_weight, preferred_element_type=jnp.float32)
    inner_act = (jax.nn.silu(gate_val) * up_val).astype(jnp.bfloat16)
    ffn_term = jnp.dot(inner_act, down_weight, preferred_element_type=jnp.float32)
    ffn_blocks = ffn_term.reshape(tokens, ctx_count, slice_width).transpose(1, 0, 2)
    ffn_cols = core_sum(jnp.sum(exchange(ffn_blocks), axis=0))
    output = (residual_cols.astype(jnp.float32) + ffn_cols).astype(jnp.bfloat16)
    out_cols = slice_width // 2
    output = lax.dynamic_slice_in_dim(output, kvh_index * out_cols, out_cols, 1)
    return output.reshape(row_count, step_count, out_cols)


def solution(mesh):
    in_specs = (
        P(),
        P(),
        P("ctx", "kvh"),
        P("ctx", "kvh"),
        P("ctx", "kvh"),
        P(None, "ctx", "kvh", None),
        P(None, "ctx", "kvh", None),
        P(),
        P(),
        P("kvh", "ctx"),
        P(),
        P(None, ("ctx", "kvh")),
        P(None, ("ctx", "kvh")),
        P(("ctx", "kvh"), None),
    )
    out_specs = P(None, None, ("ctx", "kvh"))
    return jax.shard_map(shards, mesh=mesh, in_specs=in_specs, out_specs=out_specs, check_vma=False)
```

```python
import jax
import jax.numpy as jnp
from jax import lax
from jax.experimental import pallas as pl
from jax.experimental.pallas import tpu as pltpu
from jax.sharding import PartitionSpec as P


VMEM = pl.BlockSpec(memory_space=pltpu.VMEM)
HBM = pl.BlockSpec(memory_space=pltpu.HBM)


def far(array):
    return pltpu.with_memory_space_constraint(array, pltpu.HBM)


def heads_kernel(
    hidden_any, gain_ref, q_any, k_any, v_any, out_ref, own_ref, hidden_ref, q_ref, k_ref, v_ref, sem
):
    pairs = ((hidden_any, hidden_ref), (q_any, q_ref), (k_any, k_ref), (v_any, v_ref))
    copies = [pltpu.make_async_copy(*pair, sem.at[i]) for i, pair in enumerate(pairs)]
    for copy in copies:
        copy.start()
    rows, steps, width = hidden_ref.shape
    depth, head_dim = q_ref.shape[0], out_ref.shape[2]
    index = lax.axis_index("ctx")
    own = pl.ds(pl.multiple_of(index * depth, depth), depth)
    gains = gain_ref[...].astype(jnp.float32)
    picked = lax.broadcasted_iota(jnp.int32, gains.shape, 0) == index
    gain = jnp.sum(jnp.where(picked, gains, 0.0), axis=0, keepdims=True)
    heads = (q_ref.shape[1] + k_ref.shape[1] + v_ref.shape[1]) // head_dim
    out_ref[heads:] = jnp.zeros((out_ref.shape[0] - heads,) + out_ref.shape[1:], jnp.float32)
    copies[0].wait()
    normed = []
    for row in range(rows):
        values = hidden_ref[row].astype(jnp.float32)
        spread = jnp.sum(values * values, axis=-1, keepdims=True) * (1.0 / width)
        mine = hidden_ref[row, :, own].astype(jnp.float32)
        own_ref[row * steps : (row + 1) * steps] = mine
        normed.append(mine * lax.rsqrt(spread + 1e-05) * gain)
    normed = jnp.concatenate(normed, axis=0).astype(jnp.bfloat16)
    head = 0
    for copy, weight_ref in zip(copies[1:], (q_ref, k_ref, v_ref)):
        copy.wait()
        sums = jnp.dot(normed, weight_ref[...], preferred_element_type=jnp.float32)
        for start in range(0, weight_ref.shape[1], head_dim):
            out_ref[head] = sums[:, start : start + head_dim]
            head += 1


def rotate_kernel(parts_ref, cosine_ref, sine_ref, out_ref):
    total = jnp.sum(parts_ref[...], axis=0)
    half_dim = total.shape[1] // 2
    first_half, second_half = total[:, :half_dim], total[:, half_dim:]
    cosine, sine_part = cosine_ref[...], sine_ref[...]
    done = jnp.concatenate(
        [
            first_half * cosine - second_half * sine_part,
            second_half * cosine + first_half * sine_part,
        ],
        axis=-1,
    ).astype(jnp.bfloat16)
    out_ref[...] = jnp.broadcast_to(done[None], out_ref.shape)


def combine_kernel(parts_ref, out_ref):
    parts = parts_ref[...]
    share, width = out_ref.shape[1:]
    stats = parts[:, share:]
    swapped = jnp.concatenate([stats[..., width // 2 :], stats[..., : width // 2]], axis=-1)
    lower = lax.broadcasted_iota(jnp.int32, stats.shape, 2) < width // 2
    maxima = jnp.where(lower, stats, swapped)
    totals = jnp.where(lower, swapped, stats)
    factor = jnp.exp(maxima - jnp.max(maxima, axis=0, keepdims=True))
    total_sum = jnp.sum(totals * factor, axis=0)
    out_sum = jnp.sum(parts[:, :share] * factor, axis=0)
    done = (out_sum / total_sum).astype(jnp.bfloat16)
    out_ref[...] = jnp.broadcast_to(done[None], out_ref.shape)


def estimate(size):
    return pl.CostEstimate(flops=0, bytes_accessed=size, transcendentals=0)


def ffn_kernel(residual_ref, gain_ref, gate_ref, up_ref, down_ref, out_ref, input_ref):
    blocks, tokens, block = residual_ref.shape
    width, hidden = gate_ref.shape[1], gate_ref.shape[0]
    values = residual_ref[...].astype(jnp.float32)
    spread = jnp.sum(jnp.sum(values * values, axis=0), axis=-1, keepdims=True) * (1.0 / width)
    scale = lax.rsqrt(spread + 1e-05)
    for i in range(blocks):
        cols = slice(i * block, (i + 1) * block)
        scaled = values[i] * scale * gain_ref[i : i + 1].astype(jnp.float32)
        input_ref[:, cols] = scaled.astype(jnp.bfloat16)
    gate_val = jnp.zeros((tokens, hidden), jnp.float32)
    up_val = jnp.zeros((tokens, hidden), jnp.float32)
    contract = (((1,), (1,)), ((), ()))
    step = 8 * block
    for start in range(0, width, step):
        cols = slice(start, start + step)
        part = input_ref[:, cols]
        gate_val += lax.dot_general(
            part, gate_ref[:, cols], contract, preferred_element_type=jnp.float32
        )
        up_val += lax.dot_general(
            part, up_ref[:, cols], contract, preferred_element_type=jnp.float32
        )
    inner_act = (gate_val * (1.0 / (1.0 + jnp.exp(-gate_val))) * up_val).astype(jnp.bfloat16)
    for start in range(0, width, step):
        term = jnp.dot(
            inner_act, down_ref[:, start : start + step], preferred_element_type=jnp.float32
        )
        for j in range(step // block):
            out_ref[start // block + j] = term[:, j * block : (j + 1) * block]


def rotary_tables(places, head_dim):
    half_dim = head_dim // 2
    ladder = jnp.arange(half_dim, dtype=jnp.float32) * (2.0 / head_dim)
    frequency = jnp.exp(-ladder * jnp.log(500000.0))
    angles = places[:, None] * frequency[None, :]
    return (jnp.cos(angles), jnp.sin(angles))


def exchange(blocks):
    return lax.all_to_all(blocks, "ctx", 0, 0, tiled=True)


def spread_block(block):
    ctx_count = lax.axis_size("ctx")
    return exchange(jnp.broadcast_to(block[None], (ctx_count,) + block.shape))


def core_sum(values):
    return values + lax.ppermute(values, "kvh", [(0, 1), (1, 0)])


def shards(
    hidden_in,
    attn_gain,
    q_weight,
    k_weight,
    v_weight,
    key_cache,
    value_cache,
    lengths,
    positions,
    o_weight,
    ffn_gain,
    gate_weight,
    up_weight,
    down_weight,
):
    row_count, step_count, model_width = hidden_in.shape
    tokens = row_count * step_count
    head_dim = key_cache.shape[3]
    local_kv = key_cache.shape[2]
    span_len = key_cache.shape[1]
    local_heads = q_weight.shape[1] // head_dim
    group_size = local_heads // local_kv
    slice_width = q_weight.shape[0]
    shard_index = lax.axis_index("ctx")
    kvh_index = lax.axis_index("kvh")
    ctx_count = lax.axis_size("ctx")
    half_dim = head_dim // 2

    qk_heads = local_heads + local_kv
    all_heads = qk_heads + local_kv
    head_blocks, own_input = pl.pallas_call(
        heads_kernel,
        out_shape=[
            jax.ShapeDtypeStruct((ctx_count, tokens, head_dim), jnp.float32),
            jax.ShapeDtypeStruct((tokens, slice_width), jnp.float32),
        ],
        in_specs=[HBM, VMEM, HBM, HBM, HBM],
        out_specs=[VMEM] * 2,
        scratch_shapes=[
            pltpu.VMEM(a.shape, a.dtype) for a in (hidden_in, q_weight, k_weight, v_weight)
        ]
        + [pltpu.SemaphoreType.DMA((4,))],
        compiler_params=pltpu.CompilerParams(vmem_limit_bytes=8 << 20),
    )(
        far(hidden_in),
        attn_gain.reshape(ctx_count, slice_width),
        far(q_weight),
        far(k_weight),
        far(v_weight),
    )
    head_parts = exchange(head_blocks)

    places = (
        (positions[:, None] + jnp.arange(step_count, dtype=jnp.int32)[None, :])
        .reshape(tokens)
        .astype(jnp.float32)
    )
    cosine, sine_part = rotary_tables(places, head_dim)
    turned = shard_index < qk_heads
    cosine = jnp.where(turned, cosine, 1.0)
    sine_part = jnp.where(turned, sine_part, 0.0)
    heads = exchange(
        pl.pallas_call(
            rotate_kernel,
            out_shape=jax.ShapeDtypeStruct((ctx_count, tokens, head_dim), jnp.bfloat16),
            in_specs=[VMEM] * 3,
            out_specs=VMEM,
            compiler_params=pltpu.CompilerParams(vmem_limit_bytes=4 << 20),
            cost_estimate=estimate(1 << 20),
        )(head_parts, cosine, sine_part)
    )

    queries = (
        heads[:local_heads]
        .reshape(local_kv, group_size, row_count, step_count, head_dim)
        .transpose(2, 0, 1, 3, 4)
        .reshape(row_count, local_kv, group_size * step_count, head_dim)
    )
    new_keys = (
        heads[local_heads:qk_heads]
        .reshape(local_kv, row_count, step_count, head_dim)
        .transpose(1, 2, 0, 3)
    )
    new_values = (
        heads[qk_heads:all_heads]
        .reshape(local_kv, row_count, step_count, head_dim)
        .transpose(1, 2, 0, 3)
    )

    scale_val = head_dim ** (-0.5)
    cached_scores = (
        jnp.einsum("bkmd,bckd->bkmc", queries, key_cache, preferred_element_type=jnp.float32)
        * scale_val
    )
    fresh_scores = (
        jnp.einsum("bkmd,bskd->bkms", queries, new_keys, preferred_element_type=jnp.float32)
        * scale_val
    )
    slot_ids = shard_index * span_len + jnp.arange(span_len, dtype=jnp.int32)
    cached_ok = (slot_ids[None, :] < lengths[:, None])[:, None, None, :]
    step_ids = jnp.arange(step_count, dtype=jnp.int32)
    step_of = jnp.arange(step_count * group_size, dtype=jnp.int32) % step_count
    owned_new = (lengths[:, None] + step_ids[None, :]) // span_len == shard_index
    fresh_ok = owned_new[:, None, None, :] & (
        step_ids[None, None, None, :] <= step_of[None, None, :, None]
    )
    cached_masked = jnp.where(cached_ok, cached_scores, -1e30)
    fresh_masked = jnp.where(fresh_ok, fresh_scores, -1e30)
    local_max = jnp.maximum(jnp.max(cached_masked, axis=-1), jnp.max(fresh_masked, axis=-1))
    cached_weights = jnp.where(cached_ok, jnp.exp(cached_masked - local_max[..., None]), 0.0)
    fresh_weights = jnp.where(fresh_ok, jnp.exp(fresh_masked - local_max[..., None]), 0.0)
    local_total = jnp.sum(cached_weights, axis=-1) + jnp.sum(fresh_weights, axis=-1)
    local_out = jnp.einsum(
        "bkmc,bckd->bkmd",
        cached_weights.astype(jnp.bfloat16),
        value_cache,
        preferred_element_type=jnp.float32,
    )
    local_out = local_out + jnp.einsum(
        "bkms,bskd->bkmd",
        fresh_weights.astype(jnp.bfloat16),
        new_values,
        preferred_element_type=jnp.float32,
    )

    share = local_heads * tokens // ctx_count

    def by_head(values):
        width = values.shape[-1]
        return (
            values.reshape(row_count, local_kv, group_size, step_count, width)
            .transpose(1, 2, 0, 3, 4)
            .reshape(ctx_count, share, width)
        )

    stats = jnp.concatenate(
        [
            jnp.broadcast_to(local_max[..., None], local_max.shape + (half_dim,)),
            jnp.broadcast_to(local_total[..., None], local_total.shape + (half_dim,)),
        ],
        axis=-1,
    )
    partials = exchange(jnp.concatenate([by_head(local_out), by_head(stats)], axis=1))
    attended = exchange(
        pl.pallas_call(
            combine_kernel,
            out_shape=jax.ShapeDtypeStruct((ctx_count, share, head_dim), jnp.bfloat16),
            in_specs=[VMEM],
            out_specs=VMEM,
            compiler_params=pltpu.CompilerParams(vmem_limit_bytes=4 << 20),
            cost_estimate=estimate(1 << 20),
        )(partials)
    )
    attended = (
        attended.reshape(local_heads, tokens, head_dim)
        .transpose(1, 0, 2)
        .reshape(tokens, local_heads * head_dim)
    )

    attn_cols = core_sum(jnp.dot(attended, o_weight, preferred_element_type=jnp.float32))
    residual_cols = (own_input + attn_cols).astype(jnp.bfloat16)
    residual = spread_block(residual_cols)

    ffn_blocks = pl.pallas_call(
        ffn_kernel,
        out_shape=jax.ShapeDtypeStruct((ctx_count, tokens, slice_width), jnp.float32),
        in_specs=[VMEM] * 5,
        out_specs=VMEM,
        scratch_shapes=[pltpu.VMEM((tokens, model_width), jnp.bfloat16)],
        compiler_params=pltpu.CompilerParams(vmem_limit_bytes=8 << 20),
    )(
        residual,
        ffn_gain.reshape(ctx_count, slice_width),
        gate_weight.T,
        up_weight.T,
        down_weight,
    )
    ffn_cols = core_sum(jnp.sum(exchange(ffn_blocks), axis=0))
    output = (residual_cols.astype(jnp.float32) + ffn_cols).astype(jnp.bfloat16)
    out_cols = slice_width // 2
    output = lax.dynamic_slice_in_dim(output, kvh_index * out_cols, out_cols, 1)
    return output.reshape(row_count, step_count, out_cols)


def solution(mesh):
    in_specs = (
        P(),
        P(),
        P("ctx", "kvh"),
        P("ctx", "kvh"),
        P("ctx", "kvh"),
        P(None, "ctx", "kvh", None),
        P(None, "ctx", "kvh", None),
        P(),
        P(),
        P("kvh", "ctx"),
        P(),
        P(None, ("ctx", "kvh")),
        P(None, ("ctx", "kvh")),
        P(("ctx", "kvh"), None),
    )
    out_specs = P(None, None, ("ctx", "kvh"))
    return jax.shard_map(shards, mesh=mesh, in_specs=in_specs, out_specs=out_specs, check_vma=False)
```

```python
import jax
import jax.numpy as jnp
from jax import lax
from jax.experimental import pallas as pl
from jax.experimental.pallas import tpu as pltpu
from jax.sharding import PartitionSpec as P


VMEM = pl.BlockSpec(memory_space=pltpu.VMEM)
HBM = pl.BlockSpec(memory_space=pltpu.HBM)


def far(array):
    return pltpu.with_memory_space_constraint(array, pltpu.HBM)


def heads_kernel(
    hidden_any,
    gain_any,
    q_any,
    k_any,
    v_any,
    positions_any,
    lengths_any,
    frequency_ref,
    out_ref,
    own_ref,
    cosine_ref,
    sine_ref,
    limits_ref,
    hidden_ref,
    gain_ref,
    q_ref,
    k_ref,
    v_ref,
    positions_ref,
    lengths_ref,
    sem,
):
    pairs = (
        (gain_any, gain_ref),
        (hidden_any, hidden_ref),
        (q_any, q_ref),
        (k_any, k_ref),
        (v_any, v_ref),
        (positions_any, positions_ref),
        (lengths_any, lengths_ref),
    )
    copies = [pltpu.make_async_copy(*pair, sem.at[i]) for i, pair in enumerate(pairs)]
    for copy in copies:
        copy.start()
    rows, steps, width = hidden_ref.shape
    depth, head_dim = q_ref.shape[0], out_ref.shape[2]
    index = lax.axis_index("ctx")
    own = pl.ds(pl.multiple_of(index * depth, depth), depth)
    heads = (q_ref.shape[1] + k_ref.shape[1] + v_ref.shape[1]) // head_dim
    gap = v_ref.shape[1] // head_dim
    out_ref[heads - gap :] = jnp.zeros(
        (out_ref.shape[0] - heads + gap,) + out_ref.shape[1:], jnp.float32
    )
    copies[0].wait()
    gains = gain_ref[...].astype(jnp.float32)
    picked = lax.broadcasted_iota(jnp.int32, gains.shape, 0) == index
    gain = jnp.sum(jnp.where(picked, gains, 0.0), axis=0, keepdims=True)
    copies[5].wait()
    copies[6].wait()
    token = lax.broadcasted_iota(jnp.int32, cosine_ref.shape, 0)
    place = token % steps
    for row in range(rows):
        place = place + jnp.where(token // steps == row, positions_ref[row], 0)
        limits_ref[row] = jnp.full(limits_ref.shape[1:], lengths_ref[row], jnp.int32)
    angle = place.astype(jnp.float32) * frequency_ref[...]
    turned = index < (q_ref.shape[1] + k_ref.shape[1]) // head_dim
    cosine_ref[...] = jnp.where(turned, jnp.cos(angle), 1.0)
    sine_ref[...] = jnp.where(turned, jnp.sin(angle), 0.0)
    copies[1].wait()
    normed = []
    for row in range(rows):
        values = hidden_ref[row].astype(jnp.float32)
        spread = jnp.sum(values * values, axis=-1, keepdims=True) * (1.0 / width)
        mine = hidden_ref[row, :, own].astype(jnp.float32)
        own_ref[row * steps : (row + 1) * steps] = mine
        normed.append(mine * lax.rsqrt(spread + 1e-05) * gain)
    normed = jnp.concatenate(normed, axis=0).astype(jnp.bfloat16)
    head = 0
    for copy, weight_ref in zip(copies[2:5], (q_ref, k_ref, v_ref)):
        copy.wait()
        if weight_ref is v_ref:
            head += gap
        sums = jnp.dot(normed, weight_ref[...], preferred_element_type=jnp.float32)
        for start in range(0, weight_ref.shape[1], head_dim):
            out_ref[head] = sums[:, start : start + head_dim]
            head += 1


def rotate_kernel(parts_ref, cosine_ref, sine_ref, out_ref):
    total = jnp.sum(parts_ref[...], axis=0)
    half_dim = total.shape[1] // 2
    first_half, second_half = total[:, :half_dim], total[:, half_dim:]
    cosine, sine_part = cosine_ref[...], sine_ref[...]
    done = jnp.concatenate(
        [
            first_half * cosine - second_half * sine_part,
            second_half * cosine + first_half * sine_part,
        ],
        axis=-1,
    ).astype(jnp.bfloat16)
    out_ref[...] = jnp.broadcast_to(done[None], out_ref.shape)


def attend_kernel(limits_ref, heads_ref, key_ref, value_ref, out_ref):
    rows, slots, head_dim = key_ref.shape
    states = heads_ref.shape[1] - 32
    lanes = states // 16
    half = slots // 2
    span = slots // lanes
    base = lax.axis_index("ctx") * span
    scale = head_dim ** (-0.5)
    contract = (((1,), (1,)), ((), ()))
    place = lax.broadcasted_iota(jnp.int32, (2 * states, half), 1)
    state = lax.broadcasted_iota(jnp.int32, (2 * states, half), 0)
    mine = (place % lanes) == (state % states) // 16
    place = jnp.where(mine, place + (state // states) * half, 1 << 30)
    column = lax.broadcasted_iota(jnp.int32, (states, 16), 1)
    owner = lax.broadcasted_iota(jnp.int32, (states, 16), 0)
    step = column % 2
    paired = (column < 2 * lanes) & (column // 2 == owner // 16) & (step <= owner % 2)

    def score(row):
        query = heads_ref[row, :states]
        empty = jnp.zeros_like(query)
        stacked = jnp.concatenate(
            [
                jnp.concatenate([query, empty], axis=1),
                jnp.concatenate([empty, query], axis=1),
            ],
            axis=0,
        )
        keys = jnp.concatenate([key_ref[row, :half], key_ref[row, half:]], axis=1)
        cached = lax.dot_general(stacked, keys, contract, preferred_element_type=jnp.float32)
        ahead = limits_ref[row, :1, :1] - base
        cached = jnp.where(place < ahead * lanes, cached * scale, -1e30)
        fresh = lax.dot_general(
            query,
            heads_ref[row, states : states + 16],
            contract,
            preferred_element_type=jnp.float32,
        )
        slot = ahead + step
        fresh = jnp.where(paired & (slot >= 0) & (slot < span), fresh * scale, -1e30)
        return cached, fresh

    def largest(cached, fresh):
        most = jnp.max(cached, axis=1, keepdims=True)
        most = jnp.maximum(most[:states], most[states:])
        return jnp.maximum(jnp.maximum(most, jnp.max(fresh, axis=1, keepdims=True)), -1e20)

    scores = score(0)
    most = largest(*scores)
    for row in range(rows):
        cached, fresh = scores
        if row + 1 < rows:
            scores = score(row + 1)
        cached = jnp.exp(cached - jnp.concatenate([most, most], axis=0))
        fresh = jnp.exp(fresh - most)
        sums = jnp.sum(cached, axis=1, keepdims=True)
        total = sums[:states] + sums[states:] + jnp.sum(fresh, axis=1, keepdims=True)
        shown = most
        if row + 1 < rows:
            most = largest(*scores)
        values = jnp.concatenate([value_ref[row, :half], value_ref[row, half:]], axis=1)
        both = jnp.dot(cached.astype(jnp.bfloat16), values, preferred_element_type=jnp.float32)
        out_ref[row, :, :head_dim] = (
            both[:states, :head_dim]
            + both[states:, head_dim:]
            + jnp.dot(
                fresh.astype(jnp.bfloat16),
                heads_ref[row, states + 16 :],
                preferred_element_type=jnp.float32,
            )
        )
        side = (states, head_dim // 2)
        out_ref[row, :, head_dim:] = jnp.concatenate(
            [jnp.broadcast_to(shown, side), jnp.broadcast_to(total, side)], axis=1
        )


def combine_kernel(parts_ref, out_ref):
    parts = parts_ref[...]
    share, width = out_ref.shape[1:]
    stats = parts[:, share:]
    swapped = jnp.concatenate([stats[..., width // 2 :], stats[..., : width // 2]], axis=-1)
    lower = lax.broadcasted_iota(jnp.int32, stats.shape, 2) < width // 2
    maxima = jnp.where(lower, stats, swapped)
    totals = jnp.where(lower, swapped, stats)
    factor = jnp.exp(maxima - jnp.max(maxima, axis=0, keepdims=True))
    total_sum = jnp.sum(totals * factor, axis=0)
    out_sum = jnp.sum(parts[:, :share] * factor, axis=0)
    done = (out_sum / total_sum).astype(jnp.bfloat16)
    out_ref[...] = jnp.broadcast_to(done[None], out_ref.shape)


def estimate(size):
    return pl.CostEstimate(flops=0, bytes_accessed=size, transcendentals=0)


def ffn_kernel(residual_ref, gain_ref, gate_ref, up_ref, down_ref, out_ref, input_ref):
    blocks, tokens, block = residual_ref.shape
    width, hidden = gate_ref.shape[1], gate_ref.shape[0]
    values = residual_ref[...].astype(jnp.float32)
    spread = jnp.sum(jnp.sum(values * values, axis=0), axis=-1, keepdims=True) * (1.0 / width)
    scale = lax.rsqrt(spread + 1e-05)
    for i in range(blocks):
        cols = slice(i * block, (i + 1) * block)
        scaled = values[i] * scale * gain_ref[i : i + 1].astype(jnp.float32)
        input_ref[:, cols] = scaled.astype(jnp.bfloat16)
    gate_val = jnp.zeros((tokens, hidden), jnp.float32)
    up_val = jnp.zeros((tokens, hidden), jnp.float32)
    contract = (((1,), (1,)), ((), ()))
    step = 8 * block
    for start in range(0, width, step):
        cols = slice(start, start + step)
        part = input_ref[:, cols]
        gate_val += lax.dot_general(
            part, gate_ref[:, cols], contract, preferred_element_type=jnp.float32
        )
        up_val += lax.dot_general(
            part, up_ref[:, cols], contract, preferred_element_type=jnp.float32
        )
    inner_act = (gate_val * (1.0 / (1.0 + jnp.exp(-gate_val))) * up_val).astype(jnp.bfloat16)
    for start in range(0, width, step):
        term = jnp.dot(
            inner_act, down_ref[:, start : start + step], preferred_element_type=jnp.float32
        )
        for j in range(step // block):
            out_ref[start // block + j] = term[:, j * block : (j + 1) * block]


def exchange(blocks):
    return lax.all_to_all(blocks, "ctx", 0, 0, tiled=True)


def spread_block(block):
    ctx_count = lax.axis_size("ctx")
    return exchange(jnp.broadcast_to(block[None], (ctx_count,) + block.shape))


def core_sum(values):
    return values + lax.ppermute(values, "kvh", [(0, 1), (1, 0)])


def shards(
    hidden_in,
    attn_gain,
    q_weight,
    k_weight,
    v_weight,
    key_cache,
    value_cache,
    lengths,
    positions,
    o_weight,
    ffn_gain,
    gate_weight,
    up_weight,
    down_weight,
):
    row_count, step_count, model_width = hidden_in.shape
    tokens = row_count * step_count
    head_dim = key_cache.shape[3]
    local_kv = key_cache.shape[2]
    span_len = key_cache.shape[1]
    local_heads = q_weight.shape[1] // head_dim
    slice_width = q_weight.shape[0]
    shard_index = lax.axis_index("ctx")
    kvh_index = lax.axis_index("kvh")
    ctx_count = lax.axis_size("ctx")
    half_dim = head_dim // 2

    qk_heads = local_heads + local_kv
    attn_rows = attn_gain.reshape(ctx_count, slice_width)
    ladder = jnp.arange(half_dim, dtype=jnp.float32) * (2.0 / head_dim)
    frequency = jnp.exp(-ladder * jnp.log(500000.0))
    table = jax.ShapeDtypeStruct((tokens, half_dim), jnp.float32)
    head_blocks, own_input, cosine, sine_part, limits = pl.pallas_call(
        heads_kernel,
        out_shape=[
            jax.ShapeDtypeStruct((ctx_count, tokens, head_dim), jnp.float32),
            jax.ShapeDtypeStruct((tokens, slice_width), jnp.float32),
            table,
            table,
            jax.ShapeDtypeStruct((row_count, tokens, head_dim), jnp.int32),
        ],
        in_specs=[HBM] * 7 + [VMEM],
        out_specs=[VMEM] * 5,
        scratch_shapes=[
            pltpu.VMEM(a.shape, a.dtype)
            for a in (hidden_in, attn_rows, q_weight, k_weight, v_weight)
        ]
        + [pltpu.SMEM((row_count,), jnp.int32)] * 2
        + [pltpu.SemaphoreType.DMA((7,))],
        compiler_params=pltpu.CompilerParams(vmem_limit_bytes=8 << 20),
    )(
        far(hidden_in),
        far(attn_rows),
        far(q_weight),
        far(k_weight),
        far(v_weight),
        far(positions),
        far(lengths),
        frequency[None],
    )
    head_parts = exchange(head_blocks)

    heads = exchange(
        pl.pallas_call(
            rotate_kernel,
            out_shape=jax.ShapeDtypeStruct((ctx_count, tokens, head_dim), jnp.bfloat16),
            in_specs=[VMEM] * 3,
            out_specs=VMEM,
            compiler_params=pltpu.CompilerParams(vmem_limit_bytes=4 << 20),
            cost_estimate=pl.CostEstimate(flops=60_000_000_000, bytes_accessed=60 << 20, transcendentals=1 << 20),
        )(head_parts, cosine, sine_part)
    )

    gathered = qk_heads + 3 * local_kv
    by_row = (
        heads[:gathered]
        .reshape(gathered, row_count, step_count, head_dim)
        .transpose(1, 0, 2, 3)
        .reshape(row_count, gathered * step_count, head_dim)
    )
    flat_cache = (row_count, span_len * local_kv, head_dim)
    attended_parts = pl.pallas_call(
        attend_kernel,
        out_shape=jax.ShapeDtypeStruct(
            (row_count, local_heads * step_count, 2 * head_dim), jnp.float32
        ),
        in_specs=[VMEM] * 4,
        out_specs=VMEM,
        compiler_params=pltpu.CompilerParams(vmem_limit_bytes=16 << 20),
        cost_estimate=estimate(8 << 20),
    )(limits, by_row, key_cache.reshape(flat_cache), value_cache.reshape(flat_cache))

    share = local_heads * tokens // ctx_count

    def by_head(values):
        return (
            values.reshape(row_count, local_heads, step_count, head_dim)
            .transpose(1, 0, 2, 3)
            .reshape(ctx_count, share, head_dim)
        )

    local_out, stats = attended_parts[..., :head_dim], attended_parts[..., head_dim:]
    partials = exchange(jnp.concatenate([by_head(local_out), by_head(stats)], axis=1))
    attended = exchange(
        pl.pallas_call(
            combine_kernel,
            out_shape=jax.ShapeDtypeStruct((ctx_count, share, head_dim), jnp.bfloat16),
            in_specs=[VMEM],
            out_specs=VMEM,
            compiler_params=pltpu.CompilerParams(vmem_limit_bytes=4 << 20),
            cost_estimate=estimate(1 << 20),
        )(partials)
    )
    attended = (
        attended.reshape(local_heads, tokens, head_dim)
        .transpose(1, 0, 2)
        .reshape(tokens, local_heads * head_dim)
    )

    attn_cols = core_sum(jnp.dot(attended, o_weight, preferred_element_type=jnp.float32))
    residual_cols = (own_input + attn_cols).astype(jnp.bfloat16)
    residual = spread_block(residual_cols)

    ffn_blocks = pl.pallas_call(
        ffn_kernel,
        out_shape=jax.ShapeDtypeStruct((ctx_count, tokens, slice_width), jnp.float32),
        in_specs=[VMEM] * 5,
        out_specs=VMEM,
        scratch_shapes=[pltpu.VMEM((tokens, model_width), jnp.bfloat16)],
        compiler_params=pltpu.CompilerParams(vmem_limit_bytes=8 << 20),
    )(
        residual,
        ffn_gain.reshape(ctx_count, slice_width),
        gate_weight.T,
        up_weight.T,
        down_weight,
    )
    ffn_cols = core_sum(jnp.sum(exchange(ffn_blocks), axis=0))
    output = (residual_cols.astype(jnp.float32) + ffn_cols).astype(jnp.bfloat16)
    out_cols = slice_width // 2
    output = lax.dynamic_slice_in_dim(output, kvh_index * out_cols, out_cols, 1)
    return output.reshape(row_count, step_count, out_cols)


def solution(mesh):
    in_specs = (
        P(),
        P(),
        P("ctx", "kvh"),
        P("ctx", "kvh"),
        P("ctx", "kvh"),
        P(None, "ctx", "kvh", None),
        P(None, "ctx", "kvh", None),
        P(),
        P(),
        P("kvh", "ctx"),
        P(),
        P(None, ("ctx", "kvh")),
        P(None, ("ctx", "kvh")),
        P(("ctx", "kvh"), None),
    )
    out_specs = P(None, None, ("ctx", "kvh"))
    return jax.shard_map(shards, mesh=mesh, in_specs=in_specs, out_specs=out_specs, check_vma=False)
```

```python
import jax
import jax.numpy as jnp
from jax import lax
from jax.experimental import pallas as pl
from jax.experimental.pallas import tpu as pltpu
from jax.sharding import PartitionSpec as P


VMEM = pl.BlockSpec(memory_space=pltpu.VMEM)
HBM = pl.BlockSpec(memory_space=pltpu.HBM)


def far(array):
    return pltpu.with_memory_space_constraint(array, pltpu.HBM)


def heads_kernel(
    hidden_any,
    gain_any,
    q_any,
    k_any,
    v_any,
    positions_any,
    lengths_any,
    frequency_ref,
    out_ref,
    own_ref,
    cosine_ref,
    sine_ref,
    limits_ref,
    hidden_ref,
    gain_ref,
    q_ref,
    k_ref,
    v_ref,
    positions_ref,
    lengths_ref,
    sem,
):
    pairs = (
        (gain_any, gain_ref),
        (hidden_any, hidden_ref),
        (q_any, q_ref),
        (k_any, k_ref),
        (v_any, v_ref),
        (positions_any, positions_ref),
        (lengths_any, lengths_ref),
    )
    copies = [pltpu.make_async_copy(*pair, sem.at[i]) for i, pair in enumerate(pairs)]
    for copy in copies:
        copy.start()
    rows, steps, width = hidden_ref.shape
    depth, head_dim = q_ref.shape[0], out_ref.shape[2]
    index = lax.axis_index("ctx")
    own = pl.ds(pl.multiple_of(index * depth, depth), depth)
    heads = (q_ref.shape[1] + k_ref.shape[1] + v_ref.shape[1]) // head_dim
    gap = v_ref.shape[1] // head_dim
    out_ref[heads - gap :] = jnp.zeros(
        (out_ref.shape[0] - heads + gap,) + out_ref.shape[1:], jnp.float32
    )
    copies[0].wait()
    gains = gain_ref[...].astype(jnp.float32)
    picked = lax.broadcasted_iota(jnp.int32, gains.shape, 0) == index
    gain = jnp.sum(jnp.where(picked, gains, 0.0), axis=0, keepdims=True)
    copies[5].wait()
    copies[6].wait()
    token = lax.broadcasted_iota(jnp.int32, cosine_ref.shape, 0)
    place = token % steps
    for row in range(rows):
        place = place + jnp.where(token // steps == row, positions_ref[row], 0)
        limits_ref[row] = jnp.full(limits_ref.shape[1:], lengths_ref[row], jnp.int32)
    angle = place.astype(jnp.float32) * frequency_ref[...]
    owned = lax.rem(index - FIRST + out_ref.shape[0], out_ref.shape[0])
    turned = owned < (q_ref.shape[1] + k_ref.shape[1]) // head_dim
    cosine_ref[...] = jnp.where(turned, jnp.cos(angle), 1.0)
    sine_ref[...] = jnp.where(turned, jnp.sin(angle), 0.0)
    copies[1].wait()
    normed = []
    for row in range(rows):
        values = hidden_ref[row].astype(jnp.float32)
        spread = jnp.sum(values * values, axis=-1, keepdims=True) * (1.0 / width)
        mine = hidden_ref[row, :, own].astype(jnp.float32)
        own_ref[row * steps : (row + 1) * steps] = mine
        normed.append(mine * lax.rsqrt(spread + 1e-05) * gain)
    normed = jnp.concatenate(normed, axis=0).astype(jnp.bfloat16)
    head = 0
    for copy, weight_ref in zip(copies[2:5], (q_ref, k_ref, v_ref)):
        copy.wait()
        if weight_ref is v_ref:
            head += gap
        sums = jnp.dot(normed, weight_ref[...], preferred_element_type=jnp.float32)
        for start in range(0, weight_ref.shape[1], head_dim):
            out_ref[head] = sums[:, start : start + head_dim]
            head += 1


def rotate_kernel(parts_ref, cosine_ref, sine_ref, out_ref):
    total = jnp.sum(parts_ref[...], axis=0)
    half_dim = total.shape[1] // 2
    first_half, second_half = total[:, :half_dim], total[:, half_dim:]
    cosine, sine_part = cosine_ref[...], sine_ref[...]
    done = jnp.concatenate(
        [
            first_half * cosine - second_half * sine_part,
            second_half * cosine + first_half * sine_part,
        ],
        axis=-1,
    ).astype(jnp.bfloat16)
    out_ref[...] = jnp.broadcast_to(done[None], out_ref.shape)


def attend_kernel(limits_ref, heads_ref, key_ref, value_ref, out_ref):
    rows, slots, head_dim = key_ref.shape
    states = heads_ref.shape[1] - 32
    lanes = states // 16
    half = slots // 2
    span = slots // lanes
    base = lax.axis_index("ctx") * span
    scale = head_dim ** (-0.5)
    contract = (((1,), (1,)), ((), ()))
    place = lax.broadcasted_iota(jnp.int32, (2 * states, half), 1)
    state = lax.broadcasted_iota(jnp.int32, (2 * states, half), 0)
    mine = (place % lanes) == (state % states) // 16
    place = jnp.where(mine, place + (state // states) * half, 1 << 30)
    column = lax.broadcasted_iota(jnp.int32, (states, 16), 1)
    owner = lax.broadcasted_iota(jnp.int32, (states, 16), 0)
    step = column % 2
    paired = (column < 2 * lanes) & (column // 2 == owner // 16) & (step <= owner % 2)

    def score(row):
        query = heads_ref[row, :states]
        empty = jnp.zeros_like(query)
        stacked = jnp.concatenate(
            [
                jnp.concatenate([query, empty], axis=1),
                jnp.concatenate([empty, query], axis=1),
            ],
            axis=0,
        )
        keys = jnp.concatenate([key_ref[row, :half], key_ref[row, half:]], axis=1)
        cached = lax.dot_general(stacked, keys, contract, preferred_element_type=jnp.float32)
        ahead = limits_ref[row, :1, :1] - base
        cached = jnp.where(place < ahead * lanes, cached * scale, -1e30)
        fresh = lax.dot_general(
            query,
            heads_ref[row, states : states + 16],
            contract,
            preferred_element_type=jnp.float32,
        )
        slot = ahead + step
        fresh = jnp.where(paired & (slot >= 0) & (slot < span), fresh * scale, -1e30)
        return cached, fresh

    def largest(cached, fresh):
        most = jnp.max(cached, axis=1, keepdims=True)
        most = jnp.maximum(most[:states], most[states:])
        return jnp.maximum(jnp.maximum(most, jnp.max(fresh, axis=1, keepdims=True)), -1e20)

    scores = score(0)
    most = largest(*scores)
    for row in range(rows):
        cached, fresh = scores
        if row + 1 < rows:
            scores = score(row + 1)
        cached = jnp.exp(cached - jnp.concatenate([most, most], axis=0))
        fresh = jnp.exp(fresh - most)
        sums = jnp.sum(cached, axis=1, keepdims=True)
        total = sums[:states] + sums[states:] + jnp.sum(fresh, axis=1, keepdims=True)
        shown = most
        if row + 1 < rows:
            most = largest(*scores)
        values = jnp.concatenate([value_ref[row, :half], value_ref[row, half:]], axis=1)
        both = jnp.dot(cached.astype(jnp.bfloat16), values, preferred_element_type=jnp.float32)
        out_ref[row, :, :head_dim] = (
            both[:states, :head_dim]
            + both[states:, head_dim:]
            + jnp.dot(
                fresh.astype(jnp.bfloat16),
                heads_ref[row, states + 16 :],
                preferred_element_type=jnp.float32,
            )
        )
        side = (states, head_dim // 2)
        out_ref[row, :, head_dim:] = jnp.concatenate(
            [jnp.broadcast_to(shown, side), jnp.broadcast_to(total, side)], axis=1
        )


def combine_kernel(parts_ref, out_ref):
    parts = parts_ref[...]
    share, width = out_ref.shape[1:]
    stats = parts[:, share:]
    swapped = jnp.concatenate([stats[..., width // 2 :], stats[..., : width // 2]], axis=-1)
    lower = lax.broadcasted_iota(jnp.int32, stats.shape, 2) < width // 2
    maxima = jnp.where(lower, stats, swapped)
    totals = jnp.where(lower, swapped, stats)
    factor = jnp.exp(maxima - jnp.max(maxima, axis=0, keepdims=True))
    total_sum = jnp.sum(totals * factor, axis=0)
    out_sum = jnp.sum(parts[:, :share] * factor, axis=0)
    done = (out_sum / total_sum).astype(jnp.bfloat16)
    out_ref[...] = jnp.broadcast_to(done[None], out_ref.shape)


def estimate(size):
    return pl.CostEstimate(flops=0, bytes_accessed=size, transcendentals=0)


def ffn_kernel(residual_ref, gain_ref, gate_ref, up_ref, down_ref, out_ref, input_ref):
    blocks, tokens, block = residual_ref.shape
    width, hidden = gate_ref.shape[1], gate_ref.shape[0]
    values = residual_ref[...].astype(jnp.float32)
    spread = jnp.sum(jnp.sum(values * values, axis=0), axis=-1, keepdims=True) * (1.0 / width)
    scale = lax.rsqrt(spread + 1e-05)
    for i in range(blocks):
        cols = slice(i * block, (i + 1) * block)
        scaled = values[(i - FIRST) % blocks] * scale * gain_ref[i : i + 1].astype(jnp.float32)
        input_ref[:, cols] = scaled.astype(jnp.bfloat16)
    gate_val = jnp.zeros((tokens, hidden), jnp.float32)
    up_val = jnp.zeros((tokens, hidden), jnp.float32)
    contract = (((1,), (1,)), ((), ()))
    step = 8 * block
    for start in range(0, width, step):
        cols = slice(start, start + step)
        part = input_ref[:, cols]
        gate_val += lax.dot_general(
            part, gate_ref[:, cols], contract, preferred_element_type=jnp.float32
        )
        up_val += lax.dot_general(
            part, up_ref[:, cols], contract, preferred_element_type=jnp.float32
        )
    inner_act = (gate_val * (1.0 / (1.0 + jnp.exp(-gate_val))) * up_val).astype(jnp.bfloat16)
    for start in range(0, width, step):
        term = jnp.dot(
            inner_act, down_ref[:, start : start + step], preferred_element_type=jnp.float32
        )
        for j in range(step // block):
            out_ref[(start // block + j - FIRST) % blocks] = term[:, j * block : (j + 1) * block]


FIRST = 42


def exchange(blocks):
    count = lax.axis_size("ctx")
    order = [[(i + FIRST) % count for i in range(count)]]
    return lax.all_to_all(blocks, "ctx", 0, 0, tiled=True, axis_index_groups=order)


def spread_block(block):
    ctx_count = lax.axis_size("ctx")
    return exchange(jnp.broadcast_to(block[None], (ctx_count,) + block.shape))


def core_sum(values):
    return values + lax.ppermute(values, "kvh", [(0, 1), (1, 0)])


def shards(
    hidden_in,
    attn_gain,
    q_weight,
    k_weight,
    v_weight,
    key_cache,
    value_cache,
    lengths,
    positions,
    o_weight,
    ffn_gain,
    gate_weight,
    up_weight,
    down_weight,
):
    row_count, step_count, model_width = hidden_in.shape
    tokens = row_count * step_count
    head_dim = key_cache.shape[3]
    local_kv = key_cache.shape[2]
    span_len = key_cache.shape[1]
    local_heads = q_weight.shape[1] // head_dim
    slice_width = q_weight.shape[0]
    shard_index = lax.axis_index("ctx")
    kvh_index = lax.axis_index("kvh")
    ctx_count = lax.axis_size("ctx")
    half_dim = head_dim // 2

    qk_heads = local_heads + local_kv
    attn_rows = attn_gain.reshape(ctx_count, slice_width)
    ladder = jnp.arange(half_dim, dtype=jnp.float32) * (2.0 / head_dim)
    frequency = jnp.exp(-ladder * jnp.log(500000.0))
    table = jax.ShapeDtypeStruct((tokens, half_dim), jnp.float32)
    head_blocks, own_input, cosine, sine_part, limits = pl.pallas_call(
        heads_kernel,
        out_shape=[
            jax.ShapeDtypeStruct((ctx_count, tokens, head_dim), jnp.float32),
            jax.ShapeDtypeStruct((tokens, slice_width), jnp.float32),
            table,
            table,
            jax.ShapeDtypeStruct((row_count, tokens, head_dim), jnp.int32),
        ],
        in_specs=[HBM] * 7 + [VMEM],
        out_specs=[VMEM] * 5,
        scratch_shapes=[
            pltpu.VMEM(a.shape, a.dtype)
            for a in (hidden_in, attn_rows, q_weight, k_weight, v_weight)
        ]
        + [pltpu.SMEM((row_count,), jnp.int32)] * 2
        + [pltpu.SemaphoreType.DMA((7,))],
        compiler_params=pltpu.CompilerParams(vmem_limit_bytes=8 << 20),
    )(
        far(hidden_in),
        far(attn_rows),
        far(q_weight),
        far(k_weight),
        far(v_weight),
        far(positions),
        far(lengths),
        frequency[None],
    )
    head_parts = exchange(head_blocks)

    heads = exchange(
        pl.pallas_call(
            rotate_kernel,
            out_shape=jax.ShapeDtypeStruct((ctx_count, tokens, head_dim), jnp.bfloat16),
            in_specs=[VMEM] * 3,
            out_specs=VMEM,
            compiler_params=pltpu.CompilerParams(vmem_limit_bytes=4 << 20),
            cost_estimate=pl.CostEstimate(
                flops=60_000_000_000, bytes_accessed=60 << 20, transcendentals=1 << 20
            ),
        )(head_parts, cosine, sine_part)
    )

    gathered = qk_heads + 3 * local_kv
    by_row = (
        heads[:gathered]
        .reshape(gathered, row_count, step_count, head_dim)
        .transpose(1, 0, 2, 3)
        .reshape(row_count, gathered * step_count, head_dim)
    )
    flat_cache = (row_count, span_len * local_kv, head_dim)
    attended_parts = pl.pallas_call(
        attend_kernel,
        out_shape=jax.ShapeDtypeStruct(
            (row_count, local_heads * step_count, 2 * head_dim), jnp.float32
        ),
        in_specs=[VMEM] * 4,
        out_specs=VMEM,
        compiler_params=pltpu.CompilerParams(vmem_limit_bytes=16 << 20),
        cost_estimate=estimate(8 << 20),
    )(limits, by_row, key_cache.reshape(flat_cache), value_cache.reshape(flat_cache))

    share = local_heads * tokens // ctx_count

    def by_head(values):
        return (
            values.reshape(row_count, local_heads, step_count, head_dim)
            .transpose(1, 0, 2, 3)
            .reshape(ctx_count, share, head_dim)
        )

    local_out, stats = attended_parts[..., :head_dim], attended_parts[..., head_dim:]
    partials = exchange(jnp.concatenate([by_head(local_out), by_head(stats)], axis=1))
    attended = exchange(
        pl.pallas_call(
            combine_kernel,
            out_shape=jax.ShapeDtypeStruct((ctx_count, share, head_dim), jnp.bfloat16),
            in_specs=[VMEM],
            out_specs=VMEM,
            compiler_params=pltpu.CompilerParams(vmem_limit_bytes=4 << 20),
            cost_estimate=estimate(1 << 20),
        )(partials)
    )
    attended = (
        attended.reshape(local_heads, tokens, head_dim)
        .transpose(1, 0, 2)
        .reshape(tokens, local_heads * head_dim)
    )

    attn_cols = core_sum(jnp.dot(attended, o_weight, preferred_element_type=jnp.float32))
    residual_cols = (own_input + attn_cols).astype(jnp.bfloat16)
    residual = spread_block(residual_cols)

    ffn_blocks = pl.pallas_call(
        ffn_kernel,
        out_shape=jax.ShapeDtypeStruct((ctx_count, tokens, slice_width), jnp.float32),
        in_specs=[VMEM] * 5,
        out_specs=VMEM,
        scratch_shapes=[pltpu.VMEM((tokens, model_width), jnp.bfloat16)],
        compiler_params=pltpu.CompilerParams(vmem_limit_bytes=8 << 20),
    )(
        residual,
        ffn_gain.reshape(ctx_count, slice_width),
        gate_weight.T,
        up_weight.T,
        down_weight,
    )
    ffn_cols = core_sum(jnp.sum(exchange(ffn_blocks), axis=0))
    output = (residual_cols.astype(jnp.float32) + ffn_cols).astype(jnp.bfloat16)
    out_cols = slice_width // 2
    output = lax.dynamic_slice_in_dim(output, kvh_index * out_cols, out_cols, 1)
    return output.reshape(row_count, step_count, out_cols)


def solution(mesh):
    in_specs = (
        P(),
        P(),
        P("ctx", "kvh"),
        P("ctx", "kvh"),
        P("ctx", "kvh"),
        P(None, "ctx", "kvh", None),
        P(None, "ctx", "kvh", None),
        P(),
        P(),
        P("kvh", "ctx"),
        P(),
        P(None, ("ctx", "kvh")),
        P(None, ("ctx", "kvh")),
        P(("ctx", "kvh"), None),
    )
    out_specs = P(None, None, ("ctx", "kvh"))
    return jax.shard_map(shards, mesh=mesh, in_specs=in_specs, out_specs=out_specs, check_vma=False)
```

```python
import jax
import jax.numpy as jnp
from jax import lax
from jax.experimental import pallas as pl
from jax.experimental.pallas import tpu as pltpu
from jax.sharding import PartitionSpec as P


VMEM = pl.BlockSpec(memory_space=pltpu.VMEM)
HBM = pl.BlockSpec(memory_space=pltpu.HBM)


def far(array):
    return pltpu.with_memory_space_constraint(array, pltpu.HBM)


def heads_kernel(
    hidden_any,
    gain_any,
    q_any,
    k_any,
    v_any,
    positions_any,
    lengths_any,
    frequency_ref,
    out_ref,
    own_ref,
    cosine_ref,
    sine_ref,
    limits_ref,
    hidden_ref,
    gain_ref,
    q_ref,
    k_ref,
    v_ref,
    positions_ref,
    lengths_ref,
    sem,
):
    pairs = (
        (gain_any, gain_ref),
        (hidden_any, hidden_ref),
        (q_any, q_ref),
        (k_any, k_ref),
        (v_any, v_ref),
        (positions_any, positions_ref),
        (lengths_any, lengths_ref),
    )
    copies = [pltpu.make_async_copy(*pair, sem.at[i]) for i, pair in enumerate(pairs)]
    for copy in copies:
        copy.start()
    rows, steps, width = hidden_ref.shape
    depth, head_dim = q_ref.shape[0], out_ref.shape[2]
    index = lax.axis_index("ctx")
    own = pl.ds(pl.multiple_of(index * depth, depth), depth)
    heads = (q_ref.shape[1] + k_ref.shape[1] + v_ref.shape[1]) // head_dim
    gap = v_ref.shape[1] // head_dim
    out_ref[heads - gap :] = jnp.zeros(
        (out_ref.shape[0] - heads + gap,) + out_ref.shape[1:], jnp.float32
    )
    copies[0].wait()
    gains = gain_ref[...].astype(jnp.float32)
    picked = lax.broadcasted_iota(jnp.int32, gains.shape, 0) == index
    gain = jnp.sum(jnp.where(picked, gains, 0.0), axis=0, keepdims=True)
    copies[5].wait()
    copies[6].wait()
    token = lax.broadcasted_iota(jnp.int32, cosine_ref.shape, 0)
    place = token % steps
    for row in range(rows):
        place = place + jnp.where(token // steps == row, positions_ref[row], 0)
        limits_ref[row] = jnp.full(limits_ref.shape[1:], lengths_ref[row], jnp.int32)
    angle = place.astype(jnp.float32) * frequency_ref[...]
    owned = lax.rem(index - FIRST + out_ref.shape[0], out_ref.shape[0])
    turned = owned < (q_ref.shape[1] + k_ref.shape[1]) // head_dim
    cosine_ref[...] = jnp.where(turned, jnp.cos(angle), 1.0)
    sine_ref[...] = jnp.where(turned, jnp.sin(angle), 0.0)
    copies[1].wait()
    normed = []
    for row in range(rows):
        values = hidden_ref[row].astype(jnp.float32)
        spread = jnp.sum(values * values, axis=-1, keepdims=True) * (1.0 / width)
        mine = hidden_ref[row, :, own].astype(jnp.float32)
        own_ref[row * steps : (row + 1) * steps] = mine
        normed.append(mine * lax.rsqrt(spread + 1e-05) * gain)
    normed = jnp.concatenate(normed, axis=0).astype(jnp.bfloat16)
    head = 0
    for copy, weight_ref in zip(copies[2:5], (q_ref, k_ref, v_ref)):
        copy.wait()
        if weight_ref is v_ref:
            head += gap
        sums = jnp.dot(normed, weight_ref[...], preferred_element_type=jnp.float32)
        for start in range(0, weight_ref.shape[1], head_dim):
            out_ref[head] = sums[:, start : start + head_dim]
            head += 1


def rotate_kernel(parts_ref, cosine_ref, sine_ref, out_ref):
    total = jnp.sum(parts_ref[...], axis=0)
    half_dim = total.shape[1] // 2
    first_half, second_half = total[:, :half_dim], total[:, half_dim:]
    cosine, sine_part = cosine_ref[...], sine_ref[...]
    done = jnp.concatenate(
        [
            first_half * cosine - second_half * sine_part,
            second_half * cosine + first_half * sine_part,
        ],
        axis=-1,
    ).astype(jnp.bfloat16)
    out_ref[...] = jnp.broadcast_to(done[None], out_ref.shape)


def attend_kernel(limits_ref, heads_ref, key_ref, value_ref, out_ref):
    rows, slots, head_dim = key_ref.shape
    states = heads_ref.shape[1] - 32
    lanes = states // 16
    half = slots // 2
    span = slots // lanes
    base = lax.axis_index("ctx") * span
    scale = head_dim ** (-0.5)
    contract = (((1,), (1,)), ((), ()))
    place = lax.broadcasted_iota(jnp.int32, (2 * states, half), 1)
    state = lax.broadcasted_iota(jnp.int32, (2 * states, half), 0)
    mine = (place % lanes) == (state % states) // 16
    place = jnp.where(mine, place + (state // states) * half, 1 << 30)
    column = lax.broadcasted_iota(jnp.int32, (states, 16), 1)
    owner = lax.broadcasted_iota(jnp.int32, (states, 16), 0)
    step = column % 2
    paired = (column < 2 * lanes) & (column // 2 == owner // 16) & (step <= owner % 2)

    def score(row):
        query = heads_ref[row, :states]
        empty = jnp.zeros_like(query)
        stacked = jnp.concatenate(
            [
                jnp.concatenate([query, empty], axis=1),
                jnp.concatenate([empty, query], axis=1),
            ],
            axis=0,
        )
        keys = jnp.concatenate([key_ref[row, :half], key_ref[row, half:]], axis=1)
        cached = lax.dot_general(stacked, keys, contract, preferred_element_type=jnp.float32)
        ahead = limits_ref[row, :1, :1] - base
        cached = jnp.where(place < ahead * lanes, cached * scale, -1e30)
        fresh = lax.dot_general(
            query,
            heads_ref[row, states : states + 16],
            contract,
            preferred_element_type=jnp.float32,
        )
        slot = ahead + step
        fresh = jnp.where(paired & (slot >= 0) & (slot < span), fresh * scale, -1e30)
        return cached, fresh

    def largest(cached, fresh):
        most = jnp.max(cached, axis=1, keepdims=True)
        most = jnp.maximum(most[:states], most[states:])
        return jnp.maximum(jnp.maximum(most, jnp.max(fresh, axis=1, keepdims=True)), -1e20)

    scores = score(0)
    most = largest(*scores)
    for row in range(rows):
        cached, fresh = scores
        if row + 1 < rows:
            scores = score(row + 1)
        cached = jnp.exp(cached - jnp.concatenate([most, most], axis=0))
        fresh = jnp.exp(fresh - most)
        sums = jnp.sum(cached, axis=1, keepdims=True)
        total = sums[:states] + sums[states:] + jnp.sum(fresh, axis=1, keepdims=True)
        shown = most
        if row + 1 < rows:
            most = largest(*scores)
        values = jnp.concatenate([value_ref[row, :half], value_ref[row, half:]], axis=1)
        both = jnp.dot(cached.astype(jnp.bfloat16), values, preferred_element_type=jnp.float32)
        out_ref[row, :, :head_dim] = (
            both[:states, :head_dim]
            + both[states:, head_dim:]
            + jnp.dot(
                fresh.astype(jnp.bfloat16),
                heads_ref[row, states + 16 :],
                preferred_element_type=jnp.float32,
            )
        )
        side = (states, head_dim // 2)
        out_ref[row, :, head_dim:] = jnp.concatenate(
            [jnp.broadcast_to(shown, side), jnp.broadcast_to(total, side)], axis=1
        )


def combine_kernel(parts_ref, out_ref):
    parts = parts_ref[...]
    share, width = out_ref.shape[1:]
    stats = parts[:, share:]
    swapped = jnp.concatenate([stats[..., width // 2 :], stats[..., : width // 2]], axis=-1)
    lower = lax.broadcasted_iota(jnp.int32, stats.shape, 2) < width // 2
    maxima = jnp.where(lower, stats, swapped)
    totals = jnp.where(lower, swapped, stats)
    factor = jnp.exp(maxima - jnp.max(maxima, axis=0, keepdims=True))
    total_sum = jnp.sum(totals * factor, axis=0)
    out_sum = jnp.sum(parts[:, :share] * factor, axis=0)
    done = (out_sum / total_sum).astype(jnp.bfloat16)
    out_ref[...] = jnp.broadcast_to(done[None], out_ref.shape)


def estimate(size):
    return pl.CostEstimate(flops=0, bytes_accessed=size, transcendentals=0)


def ffn_kernel(residual_ref, gain_ref, gate_ref, up_ref, down_ref, out_ref, input_ref):
    blocks, tokens, block = residual_ref.shape
    width, hidden = gate_ref.shape[1], gate_ref.shape[0]
    values = residual_ref[...].astype(jnp.float32)
    spread = jnp.sum(jnp.sum(values * values, axis=0), axis=-1, keepdims=True) * (1.0 / width)
    scale = lax.rsqrt(spread + 1e-05)
    for i in range(blocks):
        cols = slice(i * block, (i + 1) * block)
        scaled = values[(i - FIRST) % blocks] * scale * gain_ref[i : i + 1].astype(jnp.float32)
        input_ref[:, cols] = scaled.astype(jnp.bfloat16)
    gate_val = jnp.zeros((tokens, hidden), jnp.float32)
    up_val = jnp.zeros((tokens, hidden), jnp.float32)
    contract = (((1,), (1,)), ((), ()))
    step = 8 * block
    for start in range(0, width, step):
        cols = slice(start, start + step)
        part = input_ref[:, cols]
        gate_val += lax.dot_general(
            part, gate_ref[:, cols], contract, preferred_element_type=jnp.float32
        )
        up_val += lax.dot_general(
            part, up_ref[:, cols], contract, preferred_element_type=jnp.float32
        )
    inner_act = (gate_val * (1.0 / (1.0 + jnp.exp(-gate_val))) * up_val).astype(jnp.bfloat16)
    for start in range(0, width, step):
        term = jnp.dot(
            inner_act, down_ref[:, start : start + step], preferred_element_type=jnp.float32
        )
        for j in range(step // block):
            piece = term[:, j * block : (j + 1) * block].astype(out_ref.dtype)
            out_ref[(start // block + j - FIRST) % blocks] = piece


FIRST = 42


def exchange(blocks):
    count = lax.axis_size("ctx")
    order = [[(i + FIRST) % count for i in range(count)]]
    return lax.all_to_all(blocks, "ctx", 0, 0, tiled=True, axis_index_groups=order)


def spread_block(block):
    ctx_count = lax.axis_size("ctx")
    return exchange(jnp.broadcast_to(block[None], (ctx_count,) + block.shape))


def core_sum(values):
    return values + lax.ppermute(values, "kvh", [(0, 1), (1, 0)])


def shards(
    hidden_in,
    attn_gain,
    q_weight,
    k_weight,
    v_weight,
    key_cache,
    value_cache,
    lengths,
    positions,
    o_weight,
    ffn_gain,
    gate_weight,
    up_weight,
    down_weight,
):
    row_count, step_count, model_width = hidden_in.shape
    tokens = row_count * step_count
    head_dim = key_cache.shape[3]
    local_kv = key_cache.shape[2]
    span_len = key_cache.shape[1]
    local_heads = q_weight.shape[1] // head_dim
    slice_width = q_weight.shape[0]
    shard_index = lax.axis_index("ctx")
    kvh_index = lax.axis_index("kvh")
    ctx_count = lax.axis_size("ctx")
    half_dim = head_dim // 2

    qk_heads = local_heads + local_kv
    attn_rows = attn_gain.reshape(ctx_count, slice_width)
    ladder = jnp.arange(half_dim, dtype=jnp.float32) * (2.0 / head_dim)
    frequency = jnp.exp(-ladder * jnp.log(500000.0))
    table = jax.ShapeDtypeStruct((tokens, half_dim), jnp.float32)
    head_blocks, own_input, cosine, sine_part, limits = pl.pallas_call(
        heads_kernel,
        out_shape=[
            jax.ShapeDtypeStruct((ctx_count, tokens, head_dim), jnp.float32),
            jax.ShapeDtypeStruct((tokens, slice_width), jnp.float32),
            table,
            table,
            jax.ShapeDtypeStruct((row_count, tokens, head_dim), jnp.int32),
        ],
        in_specs=[HBM] * 7 + [VMEM],
        out_specs=[VMEM] * 5,
        scratch_shapes=[
            pltpu.VMEM(a.shape, a.dtype)
            for a in (hidden_in, attn_rows, q_weight, k_weight, v_weight)
        ]
        + [pltpu.SMEM((row_count,), jnp.int32)] * 2
        + [pltpu.SemaphoreType.DMA((7,))],
        compiler_params=pltpu.CompilerParams(vmem_limit_bytes=8 << 20),
    )(
        far(hidden_in),
        far(attn_rows),
        far(q_weight),
        far(k_weight),
        far(v_weight),
        far(positions),
        far(lengths),
        frequency[None],
    )
    head_parts = exchange(head_blocks)

    heads = exchange(
        pl.pallas_call(
            rotate_kernel,
            out_shape=jax.ShapeDtypeStruct((ctx_count, tokens, head_dim), jnp.bfloat16),
            in_specs=[VMEM] * 3,
            out_specs=VMEM,
            compiler_params=pltpu.CompilerParams(vmem_limit_bytes=4 << 20),
            cost_estimate=pl.CostEstimate(
                flops=60_000_000_000, bytes_accessed=60 << 20, transcendentals=1 << 20
            ),
        )(head_parts, cosine, sine_part)
    )

    gathered = qk_heads + 3 * local_kv
    by_row = (
        heads[:gathered]
        .reshape(gathered, row_count, step_count, head_dim)
        .transpose(1, 0, 2, 3)
        .reshape(row_count, gathered * step_count, head_dim)
    )
    flat_cache = (row_count, span_len * local_kv, head_dim)
    attended_parts = pl.pallas_call(
        attend_kernel,
        out_shape=jax.ShapeDtypeStruct(
            (row_count, local_heads * step_count, 2 * head_dim), jnp.float32
        ),
        in_specs=[VMEM] * 4,
        out_specs=VMEM,
        compiler_params=pltpu.CompilerParams(vmem_limit_bytes=16 << 20),
        cost_estimate=estimate(8 << 20),
    )(limits, by_row, key_cache.reshape(flat_cache), value_cache.reshape(flat_cache))

    share = local_heads * tokens // ctx_count

    def by_head(values):
        return (
            values.reshape(row_count, local_heads, step_count, head_dim)
            .transpose(1, 0, 2, 3)
            .reshape(ctx_count, share, head_dim)
        )

    local_out, stats = attended_parts[..., :head_dim], attended_parts[..., head_dim:]
    partials = exchange(jnp.concatenate([by_head(local_out), by_head(stats)], axis=1))
    attended = exchange(
        pl.pallas_call(
            combine_kernel,
            out_shape=jax.ShapeDtypeStruct((ctx_count, share, head_dim), jnp.bfloat16),
            in_specs=[VMEM],
            out_specs=VMEM,
            compiler_params=pltpu.CompilerParams(vmem_limit_bytes=4 << 20),
            cost_estimate=estimate(1 << 20),
        )(partials)
    )
    attended = (
        attended.reshape(local_heads, tokens, head_dim)
        .transpose(1, 0, 2)
        .reshape(tokens, local_heads * head_dim)
    )

    attn_cols = core_sum(jnp.dot(attended, o_weight, preferred_element_type=jnp.float32))
    residual_cols = (own_input + attn_cols).astype(jnp.bfloat16)
    residual = spread_block(residual_cols)

    ffn_blocks = pl.pallas_call(
        ffn_kernel,
        out_shape=jax.ShapeDtypeStruct((ctx_count, tokens, slice_width), jnp.bfloat16),
        in_specs=[VMEM] * 5,
        out_specs=VMEM,
        scratch_shapes=[pltpu.VMEM((tokens, model_width), jnp.bfloat16)],
        compiler_params=pltpu.CompilerParams(vmem_limit_bytes=8 << 20),
    )(
        residual,
        ffn_gain.reshape(ctx_count, slice_width),
        gate_weight.T,
        up_weight.T,
        down_weight,
    )
    ffn_cols = core_sum(jnp.sum(exchange(ffn_blocks).astype(jnp.float32), axis=0))
    output = (residual_cols.astype(jnp.float32) + ffn_cols).astype(jnp.bfloat16)
    out_cols = slice_width // 2
    output = lax.dynamic_slice_in_dim(output, kvh_index * out_cols, out_cols, 1)
    return output.reshape(row_count, step_count, out_cols)


def solution(mesh):
    in_specs = (
        P(),
        P(),
        P("ctx", "kvh"),
        P("ctx", "kvh"),
        P("ctx", "kvh"),
        P(None, "ctx", "kvh", None),
        P(None, "ctx", "kvh", None),
        P(),
        P(),
        P("kvh", "ctx"),
        P(),
        P(None, ("ctx", "kvh")),
        P(None, ("ctx", "kvh")),
        P(("ctx", "kvh"), None),
    )
    out_specs = P(None, None, ("ctx", "kvh"))
    return jax.shard_map(shards, mesh=mesh, in_specs=in_specs, out_specs=out_specs, check_vma=False)
```

```python
import jax
import jax.numpy as jnp
from jax import lax
from jax.experimental import pallas as pl
from jax.experimental.pallas import tpu as pltpu
from jax.sharding import PartitionSpec as P


VMEM = pl.BlockSpec(memory_space=pltpu.VMEM)
HBM = pl.BlockSpec(memory_space=pltpu.HBM)


def far(array):
    return pltpu.with_memory_space_constraint(array, pltpu.HBM)


def heads_kernel(
    hidden_any,
    gain_any,
    q_any,
    k_any,
    v_any,
    positions_any,
    lengths_any,
    frequency_ref,
    out_ref,
    own_ref,
    cosine_ref,
    sine_ref,
    limits_ref,
    hidden_ref,
    gain_ref,
    q_ref,
    k_ref,
    v_ref,
    positions_ref,
    lengths_ref,
    sem,
):
    pairs = (
        (gain_any, gain_ref),
        (hidden_any, hidden_ref),
        (q_any, q_ref),
        (k_any, k_ref),
        (v_any, v_ref),
        (positions_any, positions_ref),
        (lengths_any, lengths_ref),
    )
    copies = [pltpu.make_async_copy(*pair, sem.at[i]) for i, pair in enumerate(pairs)]
    for copy in copies[5:] + copies[:5]:
        copy.start()
    rows, steps, width = hidden_ref.shape
    depth, head_dim = q_ref.shape[0], out_ref.shape[2]
    index = lax.axis_index("ctx")
    own = pl.ds(pl.multiple_of(index * depth, depth), depth)
    heads = (q_ref.shape[1] + k_ref.shape[1] + v_ref.shape[1]) // head_dim
    gap = v_ref.shape[1] // head_dim
    out_ref[heads - gap :] = jnp.zeros(
        (out_ref.shape[0] - heads + gap,) + out_ref.shape[1:], jnp.float32
    )
    copies[0].wait()
    gains = gain_ref[...].astype(jnp.float32)
    picked = lax.broadcasted_iota(jnp.int32, gains.shape, 0) == index
    gain = jnp.sum(jnp.where(picked, gains, 0.0), axis=0, keepdims=True)
    copies[5].wait()
    copies[6].wait()
    token = lax.broadcasted_iota(jnp.int32, cosine_ref.shape, 0)
    place = token % steps
    for row in range(rows):
        place = place + jnp.where(token // steps == row, positions_ref[row], 0)
        limits_ref[row] = jnp.full(limits_ref.shape[1:], lengths_ref[row], jnp.int32)
    angle = place.astype(jnp.float32) * frequency_ref[...]
    owned = lax.rem(index - FIRST + out_ref.shape[0], out_ref.shape[0])
    turned = owned < (q_ref.shape[1] + k_ref.shape[1]) // head_dim
    cosine_ref[...] = jnp.where(turned, jnp.cos(angle), 1.0)
    sine_ref[...] = jnp.where(turned, jnp.sin(angle), 0.0)
    copies[1].wait()
    normed = []
    for row in range(rows):
        values = hidden_ref[row].astype(jnp.float32)
        spread = jnp.sum(values * values, axis=-1, keepdims=True) * (1.0 / width)
        mine = hidden_ref[row, :, own].astype(jnp.float32)
        own_ref[row * steps : (row + 1) * steps] = mine
        normed.append(mine * lax.rsqrt(spread + 1e-05) * gain)
    normed = jnp.concatenate(normed, axis=0).astype(jnp.bfloat16)
    head = 0
    for copy, weight_ref in zip(copies[2:5], (q_ref, k_ref, v_ref)):
        copy.wait()
        if weight_ref is v_ref:
            head += gap
        sums = jnp.dot(normed, weight_ref[...], preferred_element_type=jnp.float32)
        for start in range(0, weight_ref.shape[1], head_dim):
            out_ref[head] = sums[:, start : start + head_dim]
            head += 1


def rotate_kernel(parts_ref, cosine_ref, sine_ref, out_ref):
    total = jnp.sum(parts_ref[...], axis=0)
    half_dim = total.shape[1] // 2
    first_half, second_half = total[:, :half_dim], total[:, half_dim:]
    cosine, sine_part = cosine_ref[...], sine_ref[...]
    done = jnp.concatenate(
        [
            first_half * cosine - second_half * sine_part,
            second_half * cosine + first_half * sine_part,
        ],
        axis=-1,
    ).astype(jnp.bfloat16)
    out_ref[...] = jnp.broadcast_to(done[None], out_ref.shape)


def attend_kernel(limits_ref, heads_ref, key_ref, value_ref, out_ref):
    rows, slots, head_dim = key_ref.shape
    states = heads_ref.shape[1] - 32
    lanes = states // 16
    half = slots // 2
    span = slots // lanes
    base = lax.axis_index("ctx") * span
    scale = head_dim ** (-0.5)
    contract = (((1,), (1,)), ((), ()))
    place = lax.broadcasted_iota(jnp.int32, (2 * states, half), 1)
    state = lax.broadcasted_iota(jnp.int32, (2 * states, half), 0)
    mine = (place % lanes) == (state % states) // 16
    place = jnp.where(mine, place + (state // states) * half, 1 << 30)
    column = lax.broadcasted_iota(jnp.int32, (states, 16), 1)
    owner = lax.broadcasted_iota(jnp.int32, (states, 16), 0)
    step = column % 2
    paired = (column < 2 * lanes) & (column // 2 == owner // 16) & (step <= owner % 2)

    def score(row):
        query = heads_ref[row, :states]
        empty = jnp.zeros_like(query)
        stacked = jnp.concatenate(
            [
                jnp.concatenate([query, empty], axis=1),
                jnp.concatenate([empty, query], axis=1),
            ],
            axis=0,
        )
        keys = jnp.concatenate([key_ref[row, :half], key_ref[row, half:]], axis=1)
        cached = lax.dot_general(stacked, keys, contract, preferred_element_type=jnp.float32)
        ahead = limits_ref[row, :1, :1] - base
        cached = jnp.where(place < ahead * lanes, cached * scale, -1e30)
        fresh = lax.dot_general(
            query,
            heads_ref[row, states : states + 16],
            contract,
            preferred_element_type=jnp.float32,
        )
        slot = ahead + step
        fresh = jnp.where(paired & (slot >= 0) & (slot < span), fresh * scale, -1e30)
        return cached, fresh

    def largest(cached, fresh):
        most = jnp.max(cached, axis=1, keepdims=True)
        most = jnp.maximum(most[:states], most[states:])
        return jnp.maximum(jnp.maximum(most, jnp.max(fresh, axis=1, keepdims=True)), -1e20)

    scores = score(0)
    most = largest(*scores)
    for row in range(rows):
        cached, fresh = scores
        if row + 1 < rows:
            scores = score(row + 1)
        cached = jnp.exp(cached - jnp.concatenate([most, most], axis=0))
        fresh = jnp.exp(fresh - most)
        sums = jnp.sum(cached, axis=1, keepdims=True)
        total = sums[:states] + sums[states:] + jnp.sum(fresh, axis=1, keepdims=True)
        shown = most
        if row + 1 < rows:
            most = largest(*scores)
        values = jnp.concatenate([value_ref[row, :half], value_ref[row, half:]], axis=1)
        both = jnp.dot(cached.astype(jnp.bfloat16), values, preferred_element_type=jnp.float32)
        out_ref[row, :, :head_dim] = (
            both[:states, :head_dim]
            + both[states:, head_dim:]
            + jnp.dot(
                fresh.astype(jnp.bfloat16),
                heads_ref[row, states + 16 :],
                preferred_element_type=jnp.float32,
            )
        )
        side = (states, head_dim // 2)
        out_ref[row, :, head_dim:] = jnp.concatenate(
            [jnp.broadcast_to(shown, side), jnp.broadcast_to(total, side)], axis=1
        )


def combine_kernel(parts_ref, out_ref):
    parts = parts_ref[...]
    share, width = out_ref.shape[1:]
    stats = parts[:, share:]
    swapped = jnp.concatenate([stats[..., width // 2 :], stats[..., : width // 2]], axis=-1)
    lower = lax.broadcasted_iota(jnp.int32, stats.shape, 2) < width // 2
    maxima = jnp.where(lower, stats, swapped)
    totals = jnp.where(lower, swapped, stats)
    factor = jnp.exp(maxima - jnp.max(maxima, axis=0, keepdims=True))
    total_sum = jnp.sum(totals * factor, axis=0)
    out_sum = jnp.sum(parts[:, :share] * factor, axis=0)
    done = (out_sum / total_sum).astype(jnp.bfloat16)
    out_ref[...] = jnp.broadcast_to(done[None], out_ref.shape)


def estimate(size):
    return pl.CostEstimate(flops=0, bytes_accessed=size, transcendentals=0)


def ffn_kernel(residual_ref, gain_ref, gate_ref, up_ref, down_ref, out_ref, input_ref):
    blocks, tokens, block = residual_ref.shape
    width, hidden = gate_ref.shape[1], gate_ref.shape[0]
    values = residual_ref[...].astype(jnp.float32)
    spread = jnp.sum(jnp.sum(values * values, axis=0), axis=-1, keepdims=True) * (1.0 / width)
    scale = lax.rsqrt(spread + 1e-05)
    for i in range(blocks):
        cols = slice(i * block, (i + 1) * block)
        scaled = values[(i - FIRST) % blocks] * scale * gain_ref[i : i + 1].astype(jnp.float32)
        input_ref[:, cols] = scaled.astype(jnp.bfloat16)
    gate_val = jnp.zeros((tokens, hidden), jnp.float32)
    up_val = jnp.zeros((tokens, hidden), jnp.float32)
    contract = (((1,), (1,)), ((), ()))
    step = 8 * block
    for start in range(0, width, step):
        cols = slice(start, start + step)
        part = input_ref[:, cols]
        gate_val += lax.dot_general(
            part, gate_ref[:, cols], contract, preferred_element_type=jnp.float32
        )
        up_val += lax.dot_general(
            part, up_ref[:, cols], contract, preferred_element_type=jnp.float32
        )
    inner_act = (gate_val * (1.0 / (1.0 + jnp.exp(-gate_val))) * up_val).astype(jnp.bfloat16)
    for start in range(0, width, step):
        term = jnp.dot(
            inner_act, down_ref[:, start : start + step], preferred_element_type=jnp.float32
        )
        for j in range(step // block):
            piece = term[:, j * block : (j + 1) * block].astype(out_ref.dtype)
            out_ref[(start // block + j - FIRST) % blocks] = piece


FIRST = 42


def exchange(blocks):
    count = lax.axis_size("ctx")
    order = [[(i + FIRST) % count for i in range(count)]]
    return lax.all_to_all(blocks, "ctx", 0, 0, tiled=True, axis_index_groups=order)


def spread_block(block):
    ctx_count = lax.axis_size("ctx")
    return exchange(jnp.broadcast_to(block[None], (ctx_count,) + block.shape))


def core_sum(values):
    return values + lax.ppermute(values, "kvh", [(0, 1), (1, 0)])


def shards(
    hidden_in,
    attn_gain,
    q_weight,
    k_weight,
    v_weight,
    key_cache,
    value_cache,
    lengths,
    positions,
    o_weight,
    ffn_gain,
    gate_weight,
    up_weight,
    down_weight,
):
    row_count, step_count, model_width = hidden_in.shape
    tokens = row_count * step_count
    head_dim = key_cache.shape[3]
    local_kv = key_cache.shape[2]
    span_len = key_cache.shape[1]
    local_heads = q_weight.shape[1] // head_dim
    slice_width = q_weight.shape[0]
    shard_index = lax.axis_index("ctx")
    kvh_index = lax.axis_index("kvh")
    ctx_count = lax.axis_size("ctx")
    half_dim = head_dim // 2

    qk_heads = local_heads + local_kv
    attn_rows = attn_gain.reshape(ctx_count, slice_width)
    ladder = jnp.arange(half_dim, dtype=jnp.float32) * (2.0 / head_dim)
    frequency = jnp.exp(-ladder * jnp.log(500000.0))
    table = jax.ShapeDtypeStruct((tokens, half_dim), jnp.float32)
    head_blocks, own_input, cosine, sine_part, limits = pl.pallas_call(
        heads_kernel,
        out_shape=[
            jax.ShapeDtypeStruct((ctx_count, tokens, head_dim), jnp.float32),
            jax.ShapeDtypeStruct((tokens, slice_width), jnp.float32),
            table,
            table,
            jax.ShapeDtypeStruct((row_count, tokens, head_dim), jnp.int32),
        ],
        in_specs=[HBM] * 7 + [VMEM],
        out_specs=[VMEM] * 5,
        scratch_shapes=[
            pltpu.VMEM(a.shape, a.dtype)
            for a in (hidden_in, attn_rows, q_weight, k_weight, v_weight)
        ]
        + [pltpu.SMEM((row_count,), jnp.int32)] * 2
        + [pltpu.SemaphoreType.DMA((7,))],
        compiler_params=pltpu.CompilerParams(vmem_limit_bytes=8 << 20),
    )(
        far(hidden_in),
        far(attn_rows),
        far(q_weight),
        far(k_weight),
        far(v_weight),
        far(positions),
        far(lengths),
        frequency[None],
    )
    head_parts = exchange(head_blocks)

    heads = exchange(
        pl.pallas_call(
            rotate_kernel,
            out_shape=jax.ShapeDtypeStruct((ctx_count, tokens, head_dim), jnp.bfloat16),
            in_specs=[VMEM] * 3,
            out_specs=VMEM,
            compiler_params=pltpu.CompilerParams(vmem_limit_bytes=4 << 20),
            cost_estimate=pl.CostEstimate(
                flops=60_000_000_000, bytes_accessed=60 << 20, transcendentals=1 << 20
            ),
        )(head_parts, cosine, sine_part)
    )

    gathered = qk_heads + 3 * local_kv
    by_row = (
        heads[:gathered]
        .reshape(gathered, row_count, step_count, head_dim)
        .transpose(1, 0, 2, 3)
        .reshape(row_count, gathered * step_count, head_dim)
    )
    flat_cache = (row_count, span_len * local_kv, head_dim)
    attended_parts = pl.pallas_call(
        attend_kernel,
        out_shape=jax.ShapeDtypeStruct(
            (row_count, local_heads * step_count, 2 * head_dim), jnp.float32
        ),
        in_specs=[VMEM] * 4,
        out_specs=VMEM,
        compiler_params=pltpu.CompilerParams(vmem_limit_bytes=16 << 20),
        cost_estimate=estimate(8 << 20),
    )(limits, by_row, key_cache.reshape(flat_cache), value_cache.reshape(flat_cache))

    share = local_heads * tokens // ctx_count

    def by_head(values):
        return (
            values.reshape(row_count, local_heads, step_count, head_dim)
            .transpose(1, 0, 2, 3)
            .reshape(ctx_count, share, head_dim)
        )

    local_out, stats = attended_parts[..., :head_dim], attended_parts[..., head_dim:]
    partials = exchange(jnp.concatenate([by_head(local_out), by_head(stats)], axis=1))
    attended = exchange(
        pl.pallas_call(
            combine_kernel,
            out_shape=jax.ShapeDtypeStruct((ctx_count, share, head_dim), jnp.bfloat16),
            in_specs=[VMEM],
            out_specs=VMEM,
            compiler_params=pltpu.CompilerParams(vmem_limit_bytes=4 << 20),
            cost_estimate=estimate(1 << 20),
        )(partials)
    )
    attended = (
        attended.reshape(local_heads, tokens, head_dim)
        .transpose(1, 0, 2)
        .reshape(tokens, local_heads * head_dim)
    )

    attn_cols = core_sum(jnp.dot(attended, o_weight, preferred_element_type=jnp.float32))
    residual_cols = (own_input + attn_cols).astype(jnp.bfloat16)
    residual = spread_block(residual_cols)

    ffn_blocks = pl.pallas_call(
        ffn_kernel,
        out_shape=jax.ShapeDtypeStruct((ctx_count, tokens, slice_width), jnp.bfloat16),
        in_specs=[VMEM] * 5,
        out_specs=VMEM,
        scratch_shapes=[pltpu.VMEM((tokens, model_width), jnp.bfloat16)],
        compiler_params=pltpu.CompilerParams(vmem_limit_bytes=8 << 20),
    )(
        residual,
        ffn_gain.reshape(ctx_count, slice_width),
        gate_weight.T,
        up_weight.T,
        down_weight,
    )
    ffn_cols = core_sum(jnp.sum(exchange(ffn_blocks).astype(jnp.float32), axis=0))
    output = (residual_cols.astype(jnp.float32) + ffn_cols).astype(jnp.bfloat16)
    out_cols = slice_width // 2
    output = lax.dynamic_slice_in_dim(output, kvh_index * out_cols, out_cols, 1)
    return output.reshape(row_count, step_count, out_cols)


def solution(mesh):
    in_specs = (
        P(),
        P(),
        P("ctx", "kvh"),
        P("ctx", "kvh"),
        P("ctx", "kvh"),
        P(None, "ctx", "kvh", None),
        P(None, "ctx", "kvh", None),
        P(),
        P(),
        P("kvh", "ctx"),
        P(),
        P(None, ("ctx", "kvh")),
        P(None, ("ctx", "kvh")),
        P(("ctx", "kvh"), None),
    )
    out_specs = P(None, None, ("ctx", "kvh"))
    return jax.shard_map(shards, mesh=mesh, in_specs=in_specs, out_specs=out_specs, check_vma=False)
```
